256 devices in a mesh: bucket: 8 (over x, core), replica: 32 (over z, y).
Axes of the slice: x: 4, y: 4, z: 8, core: 2. Of those that a mesh axis runs over, the one named last changes fastest.
Arguments:
- hidden: bfloat16 [8192, 8192], P(('bucket', 'replica')), may hold values from -6 to 6
- base_query_rows: bfloat16 [8192, 4096], P(('bucket', 'replica')), may hold values from -150 to 150
- new_kv: bfloat16 [8192, 1024], P(('bucket', 'replica')), may hold values from -6 to 6
- adapter_down_matrix: bfloat16 [8192, 65536], P(None, ('bucket', 'replica')), may hold values from -0.0625 to 0.0625
- adapter_up_matrix: bfloat16 [65536, 4096], P(('bucket', 'replica')), may hold values from -0.75 to 0.75
- holder: int32 [8192, 1], P(('bucket', 'replica')), may hold values from 0 to 31; in each aligned block of 32 rows (0 to 31, 32 to 63, ...) at most 2 rows name the same one
- adapter_slot: int32 [8192], P(('bucket', 'replica')), may hold values from 0 to 3
- kv_pages: bfloat16 [24576, 16, 1024], P(('bucket', 'replica')), may hold values from -6 to 6
- mig_pages: int32 [8192], P(('bucket', 'replica')), may hold values from 0 to 95
- page_owner: int32 [32768], P(('bucket', 'replica')), may hold values from 0 to 1023, as said below
- page_used: int32 [32768], P(('bucket', 'replica')), may hold values from 1 to 16
Outputs:
- attended: bfloat16 [8192, 4096], P(('bucket', 'replica'))
The draws below stay inside these ranges and needn't reach their ends.
Inputs may be any that keep to these rules, and one draw needn't show every extreme that they name: Within each aligned block of 32 rows (the requests of one device) at most 2 rows name the same holder. `page_owner`: the 128 slots of one device are owned by exactly 2 distinct requests from each block of 32 bucket-local requests (each home replica's requests).
All inputs are finite; a program needn't handle non-finite values.
Results may differ from the reference program's by a relative error of at most 0.0065.
Values may be sent and summed in bfloat16 or wider, within the bound.
No kernel may reach another device: no remote copies, remote signals or barrier semaphores. Data moves between devices by JAX's collectives and lax.ppermute only.
A program may use at most 192 MiB of HBM per device.

```python
import math
import jax
import jax.numpy as jnp
import numpy as np
from jax import lax

D = 8192
QH = 32
KVH = 4
HD = 128
RANK = 64
ADP_DEV = 4
PAGE = 16
OWNCAP = 2
REQ_DEV = 32
RES_DEV = 96
MIGCAP = 4
QW = 4096
KVW = 512
CAP = 2
POOL = 128
GROUP_REQS = 1024
REQS = 8192
ADAPTERS = 1024
NPAGES = 24576
MIGS = 8192
POOLS = 32768
N_BUCKET = 8
N_REPLICA = 32


def draw_base_query_rows(key, part):
    values = jnp.clip(jax.random.normal(key, (REQS, QW), jnp.float32), -6.0, 6.0)
    return values.astype(jnp.bfloat16)


def draw_page_owner(key, part):
    device_count = N_BUCKET * N_REPLICA
    listed = N_REPLICA * OWNCAP
    pick_keys = jax.random.split(jax.random.fold_in(key, 11), device_count * N_REPLICA)
    picks = jax.vmap(lambda one_key: jax.random.permutation(one_key, REQ_DEV)[:OWNCAP])(pick_keys)
    picks = picks.reshape(device_count, N_REPLICA, OWNCAP).astype(jnp.int32)
    homes = jnp.arange(N_REPLICA, dtype=jnp.int32)[None, :, None]
    chosen = (homes * REQ_DEV + picks).reshape(device_count, listed)
    extra = jax.random.randint(jax.random.fold_in(key, 12), (device_count, POOL), 0, listed).astype(jnp.int32)
    slot_at = jnp.arange(POOL, dtype=jnp.int32)[None, :]
    index = jnp.where(slot_at < listed, slot_at, extra)
    spread_keys = jax.random.split(jax.random.fold_in(key, 13), device_count)
    order = jax.vmap(lambda one_key: jax.random.permutation(one_key, POOL))(spread_keys).astype(jnp.int32)
    index = jnp.take_along_axis(index, order, axis=1)
    owners = jnp.take_along_axis(chosen, index, axis=1)
    return owners.reshape(POOLS).astype(jnp.int32)


def with_ends(values, stream_key, smallest, largest):
    longest = values.shape.index(max(values.shape))
    spots = []
    for shift in (0, 1):
        where = [jax.random.randint(jax.random.fold_in(stream_key, axis), (), 0, length) for axis, length in enumerate(values.shape)]
        where[longest] = (where[longest] + shift) % values.shape[longest]
        spots.append(tuple(where))
    return values.at[spots[0]].set(smallest).at[spots[1]].set(largest)


def block_levels(own_key, shape, cuts, least, top_value):
    def one(axis_at, parts):
        steps = jax.random.uniform(jax.random.fold_in(jax.random.fold_in(own_key, 6), axis_at), (parts,), jnp.float32, least / len(cuts), top_value / len(cuts))
        return jnp.repeat(jnp.exp(steps), shape[axis_at] // parts).reshape((-1,) + (1,) * (len(shape) - axis_at - 1))

    factor_of = one(*cuts[0])
    for cut in cuts[1:]:
        factor_of = factor_of * one(*cut)
    return factor_of


def shared_out(rng, own, number, rows, amount, top, limit, skew):
    order = jax.random.permutation(rng, amount)
    crowded, ordinary = portions_of(amount, rows * top, limit, skew, True), portions_of(amount, rows * top, limit, skew, False)
    places = jnp.arange(amount)

    def named(lengths, turn):
        used = int((lengths > 0).sum())
        fixed = max(1, used // 4)
        passed = fixed + (places - fixed + turn * (used - fixed)) % max(1, amount - fixed)
        return jnp.zeros((amount,), jnp.int32).at[order[jnp.where(places < fixed, places, passed)]].set(jnp.asarray(lengths, jnp.int32))

    lengths = jnp.where(number % 4 == 0, named(crowded, number // 4), named(ordinary, number - number // 4 - 1))
    mixed = jax.random.permutation(jax.random.fold_in(own, 3), amount)
    giver, receiver = mixed[0:amount // 2 * 2:2], mixed[1:amount // 2 * 2:2]
    room = jnp.minimum(lengths[giver] - 1, limit - lengths[receiver]) // 2
    room = jnp.where((giver == order[0]) | (receiver == order[0]) | (lengths[receiver] == 0), 0, jnp.maximum(room, 0))
    passed = jax.random.randint(jax.random.fold_in(own, 4), (amount // 2,), 0, 1 << 20) % (room + 1)
    lengths = lengths.at[giver].add(-passed).at[receiver].add(passed)
    items = jnp.searchsorted(jnp.cumsum(lengths), jnp.arange(rows * top), side="right").astype(jnp.int32)
    listing = items.reshape(top, rows).T
    listing = listing[jax.random.permutation(jax.random.fold_in(own, 1), rows)]
    turn = jax.random.randint(jax.random.fold_in(own, 2), (rows, 1), 0, top)
    return jnp.take_along_axis(listing, (jnp.arange(top)[None, :] + turn) % top, axis=1)


def portions_of(number_of, total, limit, slope, full):
    portions = [(1 << 20) // math.isqrt(grade ** slope) + 1 for grade in range(1, number_of + 1)]
    largest = limit if full else min(limit, max(-(-total // number_of), total * portions[0] // sum(portions)))
    least = 1 if total - largest >= number_of - 1 else 0
    given, rest = [largest] + [least] * (number_of - 1), total - largest - least * (number_of - 1)
    while rest > 0:
        movable = [i for i in range(1, number_of) if given[i] < largest] or [i for i in range(1, number_of) if given[i] < limit]
        whole, remaining = sum([portions[i] for i in movable]), rest
        for i in movable:
            addition = min(limit - given[i], max(1, remaining * portions[i] // whole), rest)
            given[i] = given[i] + addition
            rest = rest - addition
    return np.array(given)


def gaussian(rng, shape, width, limit, pieces=(), held_as=jnp.bfloat16):
    entries = jax.random.normal(rng, shape, jnp.float32) * width
    if len(pieces) > 0:
        entries = block_levels(rng, shape, pieces, -0.22, 0.18) * entries
    return jnp.clip(entries, min=-limit, max=limit).astype(held_as)


def setup_inputs(seed: int = 0) -> dict:
    arg_keys = jax.random.split(jax.random.key(seed), 12)
    hidden = gaussian(arg_keys[0], (REQS, D), 1.0, 6.0, ((0, 256),))
    base_query_rows = draw_base_query_rows(jax.random.fold_in(arg_keys[11], 71), 0)
    new_kv = gaussian(arg_keys[2], (REQS, 2 * KVW), 1.0, 6.0, ((0, 256),))
    adapter_down_matrix = gaussian(arg_keys[3], (D, ADAPTERS * RANK), D ** -0.5, 0.0625, ((1, 256),))
    adapter_up_matrix = gaussian(arg_keys[4], (ADAPTERS * RANK, QW), RANK ** -0.5, 0.75, ((0, 256),))
    holder_keys = jax.random.split(jax.random.fold_in(arg_keys[5], 1), REQS // REQ_DEV)
    holder_turns = jax.random.permutation(jax.random.fold_in(arg_keys[5], 3), REQS // REQ_DEV)
    holder = jax.vmap(lambda own, number: shared_out(jax.random.fold_in(arg_keys[5], 2), own, number, REQ_DEV, N_REPLICA, 1, CAP, 1))(holder_keys, holder_turns).reshape((REQS, 1))
    adapter_slot = with_ends(jax.random.randint(arg_keys[6], (REQS,), 0, ADP_DEV), jax.random.fold_in(arg_keys[6], 1), 0, ADP_DEV - 1).astype(jnp.int32)
    kv_pages = gaussian(arg_keys[7], (NPAGES, PAGE, 2 * KVW), 1.0, 6.0, ((0, 256),))
    mig_pages = with_ends(jax.random.randint(arg_keys[8], (MIGS,), 0, RES_DEV), jax.random.fold_in(arg_keys[8], 1), 0, RES_DEV - 1).astype(jnp.int32)
    page_owner = draw_page_owner(jax.random.fold_in(arg_keys[11], 71), 0)
    page_used = with_ends(jax.random.randint(arg_keys[10], (POOLS,), 1, PAGE + 1), jax.random.fold_in(arg_keys[10], 1), 1, PAGE).astype(jnp.int32)
    return {"hidden": hidden, "base_query_rows": base_query_rows, "new_kv": new_kv, "adapter_down_matrix": adapter_down_matrix, "adapter_up_matrix": adapter_up_matrix, "holder": holder, "adapter_slot": adapter_slot, "kv_pages": kv_pages, "mig_pages": mig_pages, "page_owner": page_owner, "page_used": page_used}


NEG_FILL = -1e30
HIGH = lax.Precision.HIGHEST


def adapter_row_block(hidden, adapter_down_matrix, adapter_up_matrix, adapter_index_list):
    def one_request(request_item):
        row_vec, adapter_at = request_item
        down_part = lax.dynamic_slice_in_dim(adapter_down_matrix, adapter_at * RANK, RANK, 1)
        up_part = lax.dynamic_slice_in_dim(adapter_up_matrix, adapter_at * RANK, RANK, 0)
        lowered = jnp.dot(row_vec[None, :], down_part, preferred_element_type=jnp.float32).astype(jnp.bfloat16)
        return jnp.dot(lowered, up_part, preferred_element_type=jnp.float32).astype(jnp.bfloat16)[0]
    return lax.map(one_request, (hidden, adapter_index_list))


def reference(hidden, base_query_rows, new_kv, adapter_down_matrix, adapter_up_matrix, holder, adapter_slot, kv_pages, mig_pages, page_owner, page_used):
    request_ids = jnp.arange(REQS, dtype=jnp.int32)
    bucket_ids = request_ids // (REQ_DEV * N_REPLICA)
    adapter_index_list = ((bucket_ids * N_REPLICA + holder[:, 0]) * ADP_DEV + adapter_slot).astype(jnp.int32)
    low_rank_update = adapter_row_block(hidden, adapter_down_matrix, adapter_up_matrix, adapter_index_list)
    query_rows = (base_query_rows.astype(jnp.float32) + low_rank_update.astype(jnp.float32)).astype(jnp.bfloat16)
    feature = 2 * KVW
    kv_group = QH // KVH
    scale_factor = HD ** -0.5
    all_pages = kv_pages.reshape(N_BUCKET, N_REPLICA, RES_DEV, PAGE, feature)
    all_lists = mig_pages.reshape(N_BUCKET, N_REPLICA, N_BUCKET * MIGCAP)
    all_queries = query_rows.reshape(N_BUCKET, GROUP_REQS, QW)
    all_new = new_kv.reshape(N_BUCKET, GROUP_REQS, feature)
    all_owner = page_owner.reshape(N_BUCKET, N_REPLICA * POOL)
    all_used = page_used.reshape(N_BUCKET, N_REPLICA * POOL)

    def attend_bucket(bucket):
        resident = lax.dynamic_index_in_dim(all_pages, bucket, 0, keepdims=False)
        mig_lists = lax.dynamic_slice_in_dim(all_lists, (bucket * MIGCAP).astype(jnp.int32), MIGCAP, 2)
        incoming = jax.vmap(jax.vmap(lambda pages_of, picks: jnp.take(pages_of, picks, axis=0)))(all_pages, mig_lists)
        incoming = jnp.transpose(incoming, (1, 0, 2, 3, 4)).reshape(N_REPLICA, N_BUCKET * MIGCAP, PAGE, feature)
        page_pool = jnp.concatenate([resident, incoming], axis=1).reshape(N_REPLICA * POOL, PAGE, feature)
        owners = lax.dynamic_index_in_dim(all_owner, bucket, 0, keepdims=False)
        used_count = lax.dynamic_index_in_dim(all_used, bucket, 0, keepdims=False)
        group_queries = lax.dynamic_index_in_dim(all_queries, bucket, 0, keepdims=False)
        group_new = lax.dynamic_index_in_dim(all_new, bucket, 0, keepdims=False)
        picked = jnp.take(group_queries, owners, axis=0).astype(jnp.float32).reshape(-1, KVH, kv_group, HD)
        page_keys = page_pool[:, :, :KVW].astype(jnp.float32).reshape(-1, PAGE, KVH, HD)
        page_values = page_pool[:, :, KVW:].astype(jnp.float32).reshape(-1, PAGE, KVH, HD)
        scores = jnp.einsum('pkgd,ptkd->pkgt', picked, page_keys, precision=HIGH) * scale_factor
        valid_mask = (jnp.arange(PAGE)[None, :] < used_count[:, None])[:, None, None, :]
        scores = jnp.where(valid_mask, scores, NEG_FILL)
        page_top = scores.max(axis=-1)
        seg_top = jax.ops.segment_max(page_top, owners, num_segments=GROUP_REQS)
        own_queries = group_queries.astype(jnp.float32).reshape(GROUP_REQS, KVH, kv_group, HD)
        own_keys = group_new[:, :KVW].astype(jnp.float32).reshape(GROUP_REQS, KVH, HD)
        own_values = group_new[:, KVW:].astype(jnp.float32).reshape(GROUP_REQS, KVH, HD)
        own_scores = jnp.einsum('rkgd,rkd->rkg', own_queries, own_keys, precision=HIGH) * scale_factor
        highest = jnp.maximum(seg_top, own_scores)
        weights = jnp.where(valid_mask, jnp.exp(scores - jnp.take(highest, owners, axis=0)[..., None]), 0.0)
        mixed_values = jnp.einsum('pkgt,ptkd->pkgd', weights, page_values, precision=HIGH)
        own_weight = jnp.exp(own_scores - highest)
        denominator = jax.ops.segment_sum(weights.sum(axis=-1), owners, num_segments=GROUP_REQS) + own_weight
        numerator = jax.ops.segment_sum(mixed_values, owners, num_segments=GROUP_REQS) + own_weight[..., None] * own_values[:, :, None, :]
        return (numerator / denominator[..., None]).reshape(GROUP_REQS, QW).astype(jnp.bfloat16)

    result = lax.map(attend_bucket, jnp.arange(N_BUCKET, dtype=jnp.int32))
    return result.reshape(REQS, QW)
```

```python
import jax
import jax.numpy as jnp
from jax import lax
from jax.experimental import pallas as pl
from jax.experimental.pallas import tpu as pltpu
from jax.sharding import PartitionSpec as P

QH = 32
KVH = 4
HD = 128
RANK = 64
PAGE = 16
REQ = 32
NREP = 32
NBUC = 8
POOL = 128
QUART = 2048
WIDE = QUART + 128
BLOCKS = 16
CROWS = 72
SCALE = HD ** -0.5
LOW = -3e38
NEG = -1e30
HIGH = lax.Precision.HIGHEST
F32 = jnp.float32
BF16 = jnp.bfloat16
I32 = jnp.int32
VM = pl.BlockSpec(memory_space=pltpu.VMEM)
SM = pl.BlockSpec(memory_space=pltpu.SMEM)


def iota(shape, axis):
    return lax.broadcasted_iota(I32, shape, axis)


def dot_last(left, right, precision=None):
    return lax.dot_general(
        left, right, (((1,), (1,)), ((), ())), preferred_element_type=F32, precision=precision
    )


def dot(left, right, precision=None):
    return jnp.dot(left, right, preferred_element_type=F32, precision=precision)


def call(body, outs, scratch=(), ins=None, mib=12, flops=1 << 20, moved=1 << 20):
    one = not isinstance(outs, (list, tuple))
    outs = [outs] if one else list(outs)
    result = pl.pallas_call(
        body,
        out_shape=outs[0] if one else tuple(outs),
        in_specs=ins,
        out_specs=VM if one else tuple([VM] * len(outs)),
        scratch_shapes=list(scratch),
        compiler_params=pltpu.CompilerParams(vmem_limit_bytes=mib << 20),
        cost_estimate=pl.CostEstimate(flops=flops, bytes_accessed=moved, transcendentals=0),
    )
    return result


def shape(dims, kind):
    return jax.ShapeDtypeStruct(dims, kind)


def dispatch_body(hidden, holder, slot, owner, out, pos):
    col = holder[...]
    col4 = jnp.concatenate([col] * 4, axis=0)
    square = (128, 128)
    target = jnp.sum(jnp.where(iota(square, 0) == iota(square, 1), col4, 0), axis=0, keepdims=True)
    earlier = (col == target) & (iota((REQ, 128), 0) < (iota((REQ, 128), 1) & 31))
    rank = jnp.sum(jnp.where(earlier, 1, 0), axis=0, keepdims=True)
    place = 2 * target + rank
    pos[...] = place
    full = (256, 128)
    row, lane = iota(full, 0), iota(full, 1)
    at_place = (row >> 2) == place
    onehot = jnp.where(at_place & ((row & 3) == (lane >> 5)), 1.0, 0.0).astype(BF16)
    stacked = jnp.concatenate([hidden[:, q * QUART : (q + 1) * QUART] for q in range(4)], axis=0)
    out[:, :QUART] = dot(onehot, stacked).astype(BF16)
    slot_col = jnp.sum(
        jnp.where(at_place[:, :REQ], slot[...], 0), axis=1, keepdims=True
    )
    own = owner[...]
    here = (own >> 5) == (row >> 3)
    local = own & 31
    least = jnp.min(jnp.where(here, local, 99), axis=1, keepdims=True)
    most = jnp.max(jnp.where(here, local, -1), axis=1, keepdims=True)
    second = ((row >> 2) & 1) == 1
    chosen = jnp.where(second, most, least)
    meta = jnp.where(lane == 0, slot_col, jnp.where(lane == 1, chosen, 0))
    out[:, QUART:] = meta.astype(F32).astype(BF16)


def prepare_body(owner, used, rowid, spread):
    own = owner[...]
    square = (128, 128)
    row, lane = iota(square, 0), iota(square, 1)
    own_col = jnp.sum(jnp.where(row == lane, own, 0), axis=1, keepdims=True)
    least = jnp.min(jnp.where((own_col >> 5) == (own >> 5), own_col, 1 << 20), axis=0, keepdims=True)
    ids = 2 * (own >> 5) + jnp.where(own > least, 1, 0)
    rowid[...] = ids
    both = jnp.where(
        iota((16, 128), 0) == 0, ids, jnp.where(iota((16, 128), 0) == 1, used[...], 0)
    ).astype(F32).astype(BF16)
    wide = (128, POOL * PAGE)
    onehot = jnp.where(iota(wide, 0) == (iota(wide, 1) >> 4), 1.0, 0.0).astype(BF16)
    spread[...] = dot(both, onehot)[:8].astype(I32)


def leave_body(mig, pages, out, sems):
    def start(j, carry):
        pltpu.make_async_copy(pages.at[mig[0, j]], out.at[j], sems.at[j]).start()
        return carry

    def finish(j, carry):
        pltpu.make_async_copy(pages.at[0], out.at[j], sems.at[j]).wait()
        return carry

    lax.fori_loop(0, 32, start, 0)
    lax.fori_loop(0, 32, finish, 0)


def adapter_body(rows, down, up, raised, sel, spare):
    part = iota((256, 256), 0) & 3
    total = jnp.zeros((256, 256), F32)
    data = rows[:, :QUART]
    for q in range(4):
        total = jnp.where(part == q, dot(data, down[q * QUART : (q + 1) * QUART, :]), total)
    gather = jnp.where((iota((64, 256), 1) >> 2) == iota((64, 256), 0), 1.0, 0.0)
    lowered = dot(gather, total, HIGH)
    first = jnp.where(iota((64, 256), 1) == 4 * iota((64, 256), 0), 1.0, 0.0).astype(BF16)
    meta = dot(first, rows[:, QUART:]).astype(I32)
    sel[...] = jnp.sum(
        jnp.where(iota((64, 128), 0) == iota((64, 128), 1), meta[:, 1:2], 0), axis=0, keepdims=True
    )
    chosen = meta[:, 0:1] == (iota((64, 256), 1) >> 6)
    kept = jnp.where(chosen, lowered, 0.0).astype(BF16)
    for n in range(16):
        piece = dot(kept, up[:, n * 256 : (n + 1) * 256])
        spare[pl.ds(2 * n, 64, stride=32), :] = piece[:, :128]
        spare[pl.ds(2 * n + 1, 64, stride=32), :] = piece[:, 128:]
    raised[...] = spare[...].astype(BF16)


def query_body(pos, sel, delta, base, queries, out, spare):
    for h in range(QH):
        spare[pl.ds(h, REQ, stride=QH), :] = base[:, h * HD : (h + 1) * HD].astype(F32)

    def add(i, carry):
        from_row = pl.multiple_of(pos[0, i] * QH, QH)
        at = pl.multiple_of(i * QH, QH)
        moved = delta[pl.ds(from_row, QH), :].astype(F32)
        queries[pl.ds(at, QH), :] = (spare[pl.ds(at, QH), :] + moved).astype(BF16)
        return carry

    def place(c, carry):
        from_row = pl.multiple_of(sel[0, c] * QH, QH)
        out[pl.ds(pl.multiple_of(c * QH, QH), QH), :] = queries[pl.ds(from_row, QH), :]
        return carry

    lax.fori_loop(0, REQ, add, 0, unroll=8)
    lax.fori_loop(0, 2 * NREP, place, 0, unroll=8)


def own_body(queries, new_kv, own):
    lane = iota((QH, 128), 1)
    columns = jnp.zeros((QH, 128), F32)
    for i in range(REQ):
        query = queries[i * QH : (i + 1) * QH, :].astype(F32)
        keys = jnp.concatenate(
            [
                jnp.broadcast_to(new_kv[i : i + 1, g * HD : (g + 1) * HD].astype(F32), (8, HD))
                for g in range(KVH)
            ],
            axis=0,
        )
        columns = jnp.where(lane == i, jnp.sum(query * keys, axis=1, keepdims=True), columns)
    padded = jnp.concatenate([columns, jnp.zeros((96, 128), F32)], axis=0)
    own[...] = padded.T[:REQ, :] * SCALE


def group_max(values, lane):
    for step in (1, 2, 4, 8):
        up = pltpu.roll(values, step, 1)
        down = pltpu.roll(values, 128 - step, 1)
        values = jnp.maximum(values, jnp.where((lane & step) != 0, up, down))
    return values


def split3(values):
    high = values.astype(BF16).astype(F32)
    rest = values - high
    middle = rest.astype(BF16).astype(F32)
    return high, middle, rest - middle


def attend_body(rowid, spread, recv, pages, arrived, out, qf, cs, acc, spare, stats):
    qf[...] = recv[...].astype(F32)
    acc[...] = jnp.zeros_like(acc)
    lane8 = iota((8, 128), 1)
    page8 = lane8 >> 4

    def score_block(source, first):
        def step(b, carry):
            slot = (first + b) * 8
            ids = [rowid[0, slot + i] * QH for i in range(8)]
            rows = pl.ds(pl.multiple_of(b * 128, 128), 128)
            for g in range(KVH):
                query = jnp.concatenate(
                    [qf[pl.ds(pl.multiple_of(ids[i] + g * 8, 8), 8), :] for i in range(8)], axis=0
                ).astype(BF16)
                found = dot_last(query, source[rows, g * HD : (g + 1) * HD])
                kept = found[0:8]
                for i in range(1, 8):
                    kept = jnp.where(page8 == i, found[i * 8 : (i + 1) * 8], kept)
                cs[g * 8 : (g + 1) * 8, pl.ds(pl.multiple_of((first + b) * 128, 128), 128)] = kept
            return carry

        return step

    lax.fori_loop(0, 12, score_block(pages, 0), 0, unroll=2)
    lax.fori_loop(0, 4, score_block(arrived, 12), 0, unroll=2)

    lane = iota((QH, 128), 1)
    spot = lane & 15
    merged = jnp.zeros((QH, 128), F32)
    owners = jnp.zeros((QH, 128), I32)
    valid = []
    for b in range(BLOCKS):
        cut = slice(b * 128, (b + 1) * 128)
        ok = spot < spread[1:2, cut]
        valid.append(ok)
        block = jnp.where(ok, cs[:, cut] * SCALE, NEG)
        cs[:, cut] = block
        merged = jnp.where(spot == b, group_max(block, lane), merged)
        owners = jnp.where(spot == b, spread[0:1, cut], owners)

    def request(r, carry):
        tops, per_request = carry
        mine = owners == r
        top = jnp.max(jnp.where(mine, merged, LOW), axis=1, keepdims=True)
        return jnp.where(mine, top, tops), jnp.where(lane == r, top, per_request)

    zero = jnp.zeros((QH, 128), F32)
    tops, per_request = lax.fori_loop(0, 64, request, (zero, zero), unroll=8)

    sums = jnp.zeros((QH, 64), F32)
    for b in range(BLOCKS):
        cut = slice(b * 128, (b + 1) * 128)
        top = group_max(jnp.where(spot == b, tops, LOW), lane)
        weight = jnp.where(valid[b], jnp.exp(cs[:, cut] - top), 0.0).astype(BF16)
        cs[:, cut] = weight.astype(F32)
        member = jnp.where(iota((64, 128), 0) == spread[0:1, cut], 1.0, 0.0).astype(BF16)
        sums = sums + dot_last(weight, member)

    def value_block(source, first):
        def step(b, carry):
            slot = (first + b) * 8
            ids = [rowid[0, slot + i] * QH for i in range(8)]
            rows = pl.ds(pl.multiple_of(b * 128, 128), 128)
            for g in range(KVH):
                weight = cs[g * 8 : (g + 1) * 8, pl.ds(pl.multiple_of((first + b) * 128, 128), 128)]
                spreadw = jnp.concatenate(
                    [jnp.where(page8 == i, weight, 0.0) for i in range(8)], axis=0
                ).astype(BF16)
                found = dot(spreadw, source[rows, (KVH + g) * HD : (KVH + g + 1) * HD])
                for i in range(8):
                    at = pl.ds(pl.multiple_of(ids[i] + g * 8, 8), 8)
                    acc[at, :] = acc[at, :] + found[i * 8 : (i + 1) * 8]
            return carry

        return step

    lax.fori_loop(0, 12, value_block(pages, 0), 0, unroll=2)
    lax.fori_loop(0, 4, value_block(arrived, 12), 0, unroll=2)

    out[:, 0:64, :] = acc[...].astype(BF16).reshape(NREP, 64, HD)
    stats[...] = jnp.zeros_like(stats)
    whole_sums = jnp.concatenate([sums, jnp.zeros((QH, 64), F32)], axis=1)
    for k, item in enumerate((per_request, whole_sums)):
        turned = jnp.concatenate([item, jnp.zeros((96, 128), F32)], axis=0).T
        spare[...] = turned
        even = spare[pl.ds(0, 32, stride=2), :]
        odd = spare[pl.ds(1, 32, stride=2), :]
        line = even + pltpu.roll(odd, 32, 1)
        for n, piece in enumerate(split3(line)):
            stats[pl.ds(3 * k + n, 32, stride=8), :] = piece
    out[:, 64:72, :] = stats[...].astype(BF16).reshape(NREP, 8, 128)


def combine_body(sel, recv, own, new_kv, out, acc, stats, factors):
    stats[...] = recv[:, 64:72, :].astype(F32).reshape(NREP * 8, 128)

    def stat(k):
        read = [stats[pl.ds(3 * k + n, 32, stride=8), :] for n in range(3)]
        return read[0] + read[1] + read[2]

    tops, sums = stat(0), stat(1)
    tops = jnp.concatenate([tops, pltpu.roll(tops, 96, 1)], axis=0)
    sums = jnp.concatenate([sums, pltpu.roll(sums, 96, 1)], axis=0)
    lane = iota((REQ, 128), 1)
    row = iota((REQ, 128), 0)
    head = lane < QH
    own_score = jnp.where(head, own[...], 0.0)
    best = own_score
    picks = [sel[0, 2 * p + s] for s in range(2) for p in range(NREP)]
    for c in range(64):
        best = jnp.where(row == picks[c], jnp.maximum(best, tops[c : c + 1]), best)
    total = jnp.exp(own_score - best)
    for c in range(64):
        added = jnp.exp(jnp.minimum(tops[c : c + 1] - best, 0.0)) * sums[c : c + 1]
        total = total + jnp.where(row == picks[c], added, 0.0)
    inverse = 1.0 / total
    own_factor = jnp.where(head, jnp.exp(own_score - best) * inverse, 0.0)
    factors[0:32, :] = best
    factors[32:64, :] = inverse
    lines = []
    for c in range(64):
        high = factors[pl.ds(picks[c], 1), :]
        scaled = factors[pl.ds(picks[c] + 32, 1), :]
        lines.append(jnp.exp(jnp.minimum(tops[c : c + 1] - high, 0.0)) * scaled)
    turned = jnp.concatenate(lines + [own_factor, jnp.zeros((32, 128), F32)], axis=0).T
    turned = turned[:QH, :]
    for i in range(REQ):
        values = jnp.concatenate(
            [
                jnp.broadcast_to(
                    new_kv[i : i + 1, (KVH + g) * HD : (KVH + g + 1) * HD].astype(F32), (8, HD)
                )
                for g in range(KVH)
            ],
            axis=0,
        )
        acc[i * QH : (i + 1) * QH, :] = turned[:, 64 + i : 65 + i] * values
    for c in range(64):
        s, p = c // 32, c % 32
        at = pl.ds(pl.multiple_of(picks[c] * QH, QH), QH)
        given = recv[p, s * QH : (s + 1) * QH, :].astype(F32)
        acc[at, :] = acc[at, :] + turned[:, c : c + 1] * given
    for h in range(QH):
        out[:, h * HD : (h + 1) * HD] = acc[pl.ds(h, REQ, stride=QH), :].astype(BF16)


def exchange(values, axis):
    return lax.all_to_all(values, axis, split_axis=0, concat_axis=0, tiled=True)


def shards(
    hidden,
    base_query_rows,
    new_kv,
    adapter_down_matrix,
    adapter_up_matrix,
    holder,
    adapter_slot,
    kv_pages,
    mig_pages,
    page_owner,
    page_used,
):
    owner = page_owner.reshape(1, POOL)
    outgoing, pos = call(
        dispatch_body,
        [shape((256, WIDE), BF16), shape((1, 128), I32)],
        ins=[VM] * 4,
        moved=2 << 20,
    )(hidden, holder, adapter_slot.reshape(1, REQ), owner)
    rows_in = exchange(outgoing.reshape(NREP, 8, WIDE), "replica")

    leaving = pl.pallas_call(
        leave_body,
        out_shape=shape((32, PAGE, 1024), BF16),
        in_specs=[SM, pl.BlockSpec(memory_space=pl.ANY)],
        out_specs=pl.BlockSpec(memory_space=pl.ANY),
        scratch_shapes=[pltpu.SemaphoreType.DMA((32,))],
        cost_estimate=pl.CostEstimate(flops=0, bytes_accessed=2 << 20, transcendentals=0),
    )(mig_pages.reshape(1, 32), kv_pages)
    arrived = exchange(leaving.reshape(NBUC, 64, 1024), "bucket")
    rowid, spread = call(
        prepare_body,
        [shape((1, 128), I32), shape((8, POOL * PAGE), I32)],
        ins=[VM] * 2,
    )(owner, page_used.reshape(1, POOL))

    raised, sel = call(
        adapter_body,
        [shape((2048, 128), BF16), shape((1, 128), I32)],
        scratch=[pltpu.VMEM((2048, 128), F32)],
        ins=[VM] * 3,
        mib=16,
        flops=1 << 30,
        moved=8 << 20,
    )(rows_in.reshape(256, WIDE), adapter_down_matrix, adapter_up_matrix)
    returned = exchange(raised.reshape(NREP, 64, 128), "replica")

    queries, asked = call(
        query_body,
        [shape((REQ * QH, HD), BF16), shape((2048, 128), BF16)],
        scratch=[pltpu.VMEM((REQ * QH, HD), F32)],
        ins=[SM, SM, VM, VM],
    )(pos, sel, returned.reshape(2048, 128), base_query_rows)
    recv = exchange(asked.reshape(NREP, 64, 128), "replica")
    own = call(own_body, shape((REQ, 128), F32), ins=[VM] * 2)(queries, new_kv)

    partial = call(
        attend_body,
        shape((NREP, CROWS, 128), BF16),
        scratch=[
            pltpu.VMEM((2048, 128), F32),
            pltpu.VMEM((QH, POOL * PAGE), F32),
            pltpu.VMEM((2048, 128), F32),
            pltpu.VMEM((128, 128), F32),
            pltpu.VMEM((256, 128), F32),
        ],
        ins=[SM, VM, VM, VM, VM],
        mib=20,
        flops=1 << 29,
        moved=6 << 20,
    )(
        rowid,
        spread,
        recv.reshape(2048, 128),
        kv_pages.reshape(96 * PAGE, 1024),
        arrived.reshape(32 * PAGE, 1024),
    )
    parts = exchange(partial, "replica")

    return call(
        combine_body,
        shape((REQ, QH * HD), BF16),
        scratch=[
            pltpu.VMEM((REQ * QH, HD), F32),
            pltpu.VMEM((256, 128), F32),
            pltpu.VMEM((64, 128), F32),
        ],
        ins=[SM, VM, VM, VM],
    )(sel, parts, own, new_kv)


def solution(mesh):
    rows = P(("bucket", "replica"), None)
    flat = P(("bucket", "replica"))
    placed = (
        rows,
        rows,
        rows,
        P(None, ("bucket", "replica")),
        rows,
        rows,
        flat,
        P(("bucket", "replica"), None, None),
        flat,
        flat,
        flat,
    )
    return jax.shard_map(
        shards, mesh=mesh, in_specs=placed, out_specs=rows, check_vma=False
    )
```

```python
import jax
import jax.numpy as jnp
from jax import lax
from jax.experimental import pallas as pl
from jax.experimental.pallas import tpu as pltpu
from jax.sharding import PartitionSpec as P

QH = 32
KVH = 4
HD = 128
RANK = 64
PAGE = 16
REQ = 32
NREP = 32
NBUC = 8
POOL = 128
QUART = 2048
WIDE = QUART + 128
BLOCKS = 16
CROWS = 72
SCALE = HD ** -0.5
LOW = -3e38
NEG = -1e30
HIGH = lax.Precision.HIGHEST
F32 = jnp.float32
BF16 = jnp.bfloat16
I32 = jnp.int32
VM = pl.BlockSpec(memory_space=pltpu.VMEM)
ANY = pl.BlockSpec(memory_space=pl.ANY)
SM = pl.BlockSpec(memory_space=pltpu.SMEM)


def iota(shape, axis):
    return lax.broadcasted_iota(I32, shape, axis)


def dot(left, right, precision=None):
    return jnp.dot(left, right, preferred_element_type=F32, precision=precision)


def call(body, outs, scratch=(), ins=None, out_specs=None, mib=8, flops=1 << 20, moved=1 << 20):
    return pl.pallas_call(
        body,
        out_shape=tuple(outs),
        in_specs=ins,
        out_specs=tuple(out_specs or [VM] * len(outs)),
        scratch_shapes=list(scratch),
        compiler_params=pltpu.CompilerParams(vmem_limit_bytes=mib << 20),
        cost_estimate=pl.CostEstimate(flops=flops, bytes_accessed=moved, transcendentals=0),
    )


def in_hbm(values):
    return pltpu.with_memory_space_constraint(values, pltpu.HBM)


def in_vmem(values):
    return pltpu.with_memory_space_constraint(values, pltpu.VMEM)


def begin(source, target, sem):
    copy = pltpu.make_async_copy(source, target, sem)
    copy.start()
    return copy


def sems(count):
    return pltpu.SemaphoreType.DMA((count,))


def shape(dims, kind):
    return jax.ShapeDtypeStruct(dims, kind)


def dispatch_body(hidden_in, holder_in, slot_in, owner_in, out, pos, hidden, holder, slot, owner, made, sem):
    small = [
        begin(source, target, sem.at[n])
        for n, (source, target) in enumerate(
            ((holder_in, holder), (slot_in, slot), (owner_in, owner))
        )
    ]
    large = begin(hidden_in, hidden, sem.at[3])
    for copy in small:
        copy.wait()
    square = (REQ, REQ)
    col = jnp.sum(
        jnp.where(iota(square, 0) == iota(square, 1), holder[...], 0), axis=1, keepdims=True
    )
    col4 = jnp.concatenate([col] * 4, axis=0)
    square = (128, 128)
    target = jnp.sum(jnp.where(iota(square, 0) == iota(square, 1), col4, 0), axis=0, keepdims=True)
    earlier = (col == target) & (iota((REQ, 128), 0) < (iota((REQ, 128), 1) & 31))
    rank = jnp.sum(jnp.where(earlier, 1, 0), axis=0, keepdims=True)
    place = 2 * target + rank
    pos[...] = place
    full = (256, 128)
    row, lane = iota(full, 0), iota(full, 1)
    at_place = (row >> 2) == place
    onehot = jnp.where(at_place & ((row & 3) == (lane >> 5)), 1.0, 0.0).astype(BF16)
    slot_col = jnp.sum(jnp.where(at_place[:, :REQ], slot[...], 0), axis=1, keepdims=True)
    own = owner[...]
    here = (own >> 5) == (row >> 3)
    local = own & 31
    least = jnp.min(jnp.where(here, local, 99), axis=1, keepdims=True)
    most = jnp.max(jnp.where(here, local, -1), axis=1, keepdims=True)
    second = ((row >> 2) & 1) == 1
    chosen = jnp.where(second, most, least)
    meta = jnp.where(lane == 0, slot_col, jnp.where(lane == 1, chosen, 0))
    made[:, QUART:] = meta.astype(F32).astype(BF16)
    large.wait()
    stacked = jnp.concatenate([hidden[:, q * QUART : (q + 1) * QUART] for q in range(4)], axis=0)
    copies = []
    for n in range(4):
        rows = slice(n * 64, (n + 1) * 64)
        made[rows, :QUART] = dot(onehot[rows], stacked).astype(BF16)
        copies.append(begin(made.at[n * 64 : (n + 1) * 64], out.at[n * 64 : (n + 1) * 64], sem.at[4 + n]))
    for copy in copies:
        copy.wait()


def prepare_body(owner_in, used_in, pages_in, after, *rest):
    given, (rowid, spread, member, keys, values_out) = rest[:NBUC], rest[NBUC : NBUC + 5]
    owner, used, pages, pieces, values, sem = rest[NBUC + 5 :]
    copies = [
        begin(source, target, sem.at[n])
        for n, (source, target) in enumerate(
            ((owner_in, owner), (used_in, used), (pages_in, pages))
        )
    ]
    arrived = [pieces.at[k * 64 : (k + 1) * 64] for k in range(NBUC)]
    copies += [begin(given[k], arrived[k], sem.at[3 + k]) for k in range(NBUC)]
    copies[0].wait()
    copies[1].wait()
    own = owner[...]
    square = (128, 128)
    row, lane = iota(square, 0), iota(square, 1)
    own_col = jnp.sum(jnp.where(row == lane, own, 0), axis=1, keepdims=True)
    least = jnp.min(jnp.where((own_col >> 5) == (own >> 5), own_col, 1 << 20), axis=0, keepdims=True)
    ids = 2 * (own >> 5) + jnp.where(own > least, 1, 0)
    both = jnp.where(
        iota((16, 128), 0) == 0, ids, jnp.where(iota((16, 128), 0) == 1, used[...], 0)
    ).astype(F32).astype(BF16)
    turn = lax.axis_index("bucket") << 2

    def moved(slot):
        return jnp.where(slot < 96, slot, slot ^ turn)

    one = jnp.where(row == moved(lane), 1.0, 0.0).astype(BF16)
    rowid[...] = dot(both, one)[:1].astype(I32)
    wide = (128, POOL * PAGE)
    onehot = jnp.where(iota(wide, 0) == moved(iota(wide, 1) >> 4), 1.0, 0.0).astype(BF16)
    spread[...] = dot(both, onehot)[:8].astype(I32)
    tall = (POOL * PAGE, 128)
    onehot = jnp.where(iota(tall, 1) == moved(iota(tall, 0) >> 4), 1.0, 0.0).astype(BF16)
    ids_col = jnp.sum(jnp.where(row == lane, ids, 0), axis=1, keepdims=True)
    member[...] = dot(onehot, jnp.where(ids_col == lane, 1.0, 0.0).astype(BF16)).astype(BF16)
    for copy in copies[2:]:
        copy.wait()
    for b in range(12):
        rows = slice(b * 128, (b + 1) * 128)
        values[rows, :] = pages[rows, KVH * HD :]
    for k in range(NBUC):
        values[(24 + k) * 64 : (25 + k) * 64, :] = arrived[k][:, KVH * HD :]
    store = begin(values, values_out, sem.at[11])
    for b in range(BLOCKS):
        for g in range(KVH):
            cut = slice(g * HD, (g + 1) * HD)
            if b < 12:
                block = pages[b * 128 : (b + 1) * 128, cut]
            else:
                block = jnp.concatenate([one[:, cut] for one in arrived[2 * b - 24 : 2 * b - 22]], axis=0)
            keys[(b * KVH + g) * HD : (b * KVH + g + 1) * HD, :] = block.T
    store.wait()


def leave_body(mig, pages, up_in, after, *rest):
    outs, (up, sem) = rest[:NBUC], rest[NBUC:]
    me = lax.axis_index("bucket")
    copies = []
    for k in range(NBUC):
        for j in range(4):
            page = mig[0, (me ^ k) * 4 + j]
            copies.append(
                begin(
                    pages.at[pl.ds(pl.multiple_of(page * PAGE, PAGE), PAGE)],
                    outs[k].at[pl.ds(j * PAGE, PAGE)],
                    sem.at[k * 4 + j],
                )
            )
    copies.append(begin(up_in, up, sem.at[32]))
    for copy in copies:
        copy.wait()


def adapter_body(rows, down_in, up, *rest):
    raised, sel, spare, packed, down, sem = rest[NBUC:]
    loads = [
        begin(down_in.at[n * 1024 : (n + 1) * 1024], down.at[n * 1024 : (n + 1) * 1024], sem.at[4 + n])
        for n in range(8)
    ]
    part = iota((256, 256), 0) & 3
    total = jnp.zeros((256, 256), F32)
    for n in range(8):
        loads[n].wait()
        half = slice((n & 1) * 1024, (n & 1) * 1024 + 1024)
        found = dot(rows[:, half], down[n * 1024 : (n + 1) * 1024, :])
        total = total + jnp.where(part == n // 2, found, 0.0)
    gather = jnp.where((iota((64, 256), 1) >> 2) == iota((64, 256), 0), 1.0, 0.0)
    lowered = dot(gather, total, HIGH)
    first = jnp.where(iota((64, 256), 1) == 4 * iota((64, 256), 0), 1.0, 0.0).astype(BF16)
    meta = dot(first, rows[:, QUART:]).astype(I32)
    sel[...] = jnp.sum(
        jnp.where(iota((64, 128), 0) == iota((64, 128), 1), meta[:, 1:2], 0), axis=0, keepdims=True
    )
    chosen = meta[:, 0:1] == (iota((64, 256), 1) >> 6)
    kept = jnp.where(chosen, lowered, 0.0).astype(BF16)
    for n in range(16):
        piece = dot(kept, up[:, n * 256 : (n + 1) * 256])
        spare[pl.ds(2 * n, 64, stride=32), :] = piece[:, :128]
        spare[pl.ds(2 * n + 1, 64, stride=32), :] = piece[:, 128:]
    copies = []
    for n in range(4):
        packed[n * 512 : (n + 1) * 512, :] = spare[n * 512 : (n + 1) * 512, :].astype(BF16)
        copies.append(
            begin(packed.at[n * 512 : (n + 1) * 512], raised.at[n * 512 : (n + 1) * 512], sem.at[n])
        )
    for copy in copies:
        copy.wait()


def query_body(pos, sel, delta, base_in, after, queries, out, base, spare, packed, sem):
    begin(base_in, base, sem.at[4]).wait()
    for h in range(QH):
        spare[pl.ds(h, REQ, stride=QH), :] = base[:, h * HD : (h + 1) * HD].astype(F32)
    for i in range(REQ):
        from_row = pl.multiple_of(pos[0, i] * QH, QH)
        rows = slice(i * QH, (i + 1) * QH)
        queries[rows, :] = (spare[rows, :] + delta[pl.ds(from_row, QH), :].astype(F32)).astype(BF16)
    copies = []
    for c in range(2 * NREP):
        from_row = pl.multiple_of(sel[0, c] * QH, QH)
        packed[c * QH : (c + 1) * QH, :] = queries[pl.ds(from_row, QH), :]
        if c % 16 == 15:
            n = c // 16
            copies.append(
                begin(packed.at[n * 512 : (n + 1) * 512], out.at[n * 512 : (n + 1) * 512], sem.at[n])
            )
    for copy in copies:
        copy.wait()


def own_body(queries, new_in, own, new_kv, sem):
    begin(new_in, new_kv, sem.at[0]).wait()
    lane = iota((QH, 128), 1)
    columns = jnp.zeros((QH, 128), F32)
    for i in range(REQ):
        query = queries[i * QH : (i + 1) * QH, :].astype(F32)
        keys = jnp.concatenate(
            [
                jnp.broadcast_to(new_kv[i : i + 1, g * HD : (g + 1) * HD].astype(F32), (8, HD))
                for g in range(KVH)
            ],
            axis=0,
        )
        columns = jnp.where(lane == i, jnp.sum(query * keys, axis=1, keepdims=True), columns)
    padded = jnp.concatenate([columns, jnp.zeros((96, 128), F32)], axis=0)
    own[...] = padded.T[:REQ, :] * SCALE


def group_max(values, lane):
    for step in (1, 2, 4, 8):
        up = pltpu.roll(values, step, 1)
        down = pltpu.roll(values, 128 - step, 1)
        values = jnp.maximum(values, jnp.where((lane & step) != 0, up, down))
    return values


def split3(values):
    high = values.astype(BF16).astype(F32)
    rest = values - high
    middle = rest.astype(BF16).astype(F32)
    return high, middle, rest - middle


def attend_body(
    rowid, spread, member, recv, keys, values_in, out, qf, cs, acc, spare, stats, packed, values, sem
):
    load = begin(values_in, values, sem.at[4])
    qf[...] = recv[...].astype(F32)
    acc[...] = jnp.zeros_like(acc)
    lane8 = iota((8, 128), 1)
    page8 = lane8 >> 4

    def cut_of(b):
        return pl.ds(pl.multiple_of(b * 128, 128), 128)

    def score_block(b, carry):
        ids = [rowid[0, b * 8 + i] * QH for i in range(8)]
        for g in range(KVH):
            query = jnp.concatenate(
                [qf[pl.ds(pl.multiple_of(ids[i] + g * 8, 8), 8), :] for i in range(8)], axis=0
            ).astype(BF16)
            at = pl.multiple_of((b * KVH + g) * HD, HD)
            found = dot(query, keys[pl.ds(at, HD), :])
            kept = found[0:8]
            for i in range(1, 8):
                kept = jnp.where(page8 == i, found[i * 8 : (i + 1) * 8], kept)
            cs[g * 8 : (g + 1) * 8, cut_of(b)] = kept
        return carry

    lax.fori_loop(0, BLOCKS, score_block, 0, unroll=2)

    lane = iota((QH, 128), 1)
    spot = lane & 15
    merged = jnp.zeros((QH, 128), F32)
    owners = jnp.zeros((QH, 128), I32)
    valid = []
    for b in range(BLOCKS):
        cut = slice(b * 128, (b + 1) * 128)
        ok = spot < spread[1:2, cut]
        valid.append(ok)
        block = jnp.where(ok, cs[:, cut] * SCALE, NEG)
        cs[:, cut] = block
        merged = jnp.where(spot == b, group_max(block, lane), merged)
        owners = jnp.where(spot == b, spread[0:1, cut], owners)

    def request(r, carry):
        tops, per_request = carry
        mine = owners == r
        top = jnp.max(jnp.where(mine, merged, LOW), axis=1, keepdims=True)
        return jnp.where(mine, top, tops), jnp.where(lane == r, top, per_request)

    zero = jnp.zeros((QH, 128), F32)
    tops, per_request = lax.fori_loop(0, 64, request, (zero, zero), unroll=8)

    sums = jnp.zeros((QH, 128), F32)
    for b in range(BLOCKS):
        cut = slice(b * 128, (b + 1) * 128)
        top = group_max(jnp.where(spot == b, tops, LOW), lane)
        weight = jnp.where(valid[b], jnp.exp(cs[:, cut] - top), 0.0).astype(BF16)
        cs[:, cut] = weight.astype(F32)
        sums = sums + dot(weight, member[cut, :])

    def value_block(b, carry):
        ids = [rowid[0, b * 8 + i] * QH for i in range(8)]
        for g in range(KVH):
            weight = cs[g * 8 : (g + 1) * 8, cut_of(b)]
            spreadw = jnp.concatenate(
                [jnp.where(page8 == i, weight, 0.0) for i in range(8)], axis=0
            ).astype(BF16)
            found = dot(spreadw, values[cut_of(b), g * HD : (g + 1) * HD])
            for i in range(8):
                at = pl.ds(pl.multiple_of(ids[i] + g * 8, 8), 8)
                acc[at, :] = acc[at, :] + found[i * 8 : (i + 1) * 8]
        return carry

    load.wait()
    lax.fori_loop(0, BLOCKS, value_block, 0, unroll=2)

    stats[...] = jnp.zeros_like(stats)
    for k, item in enumerate((per_request, sums)):
        turned = jnp.concatenate([item, jnp.zeros((96, 128), F32)], axis=0).T
        spare[...] = turned
        even = spare[pl.ds(0, 32, stride=2), :]
        odd = spare[pl.ds(1, 32, stride=2), :]
        line = even + pltpu.roll(odd, 32, 1)
        for n, piece in enumerate(split3(line)):
            stats[pl.ds(3 * k + n, 32, stride=8), :] = piece
    packed[:, 64:72, :] = stats[...].astype(BF16).reshape(NREP, 8, 128)
    copies = []
    for n in range(4):
        part = acc[n * 512 : (n + 1) * 512, :].astype(BF16).reshape(8, 64, HD)
        packed[n * 8 : (n + 1) * 8, 0:64, :] = part
        copies.append(
            begin(packed.at[n * 8 : (n + 1) * 8], out.at[n * 8 : (n + 1) * 8], sem.at[n])
        )
    for copy in copies:
        copy.wait()


def combine_body(sel, recv, own, new_kv, out, acc, stats, factors):
    stats[...] = recv[:, 64:72, :].astype(F32).reshape(NREP * 8, 128)

    def stat(k):
        read = [stats[pl.ds(3 * k + n, 32, stride=8), :] for n in range(3)]
        return read[0] + read[1] + read[2]

    tops, sums = stat(0), stat(1)
    tops = jnp.concatenate([tops, pltpu.roll(tops, 96, 1)], axis=0)
    sums = jnp.concatenate([sums, pltpu.roll(sums, 96, 1)], axis=0)
    lane = iota((REQ, 128), 1)
    row = iota((REQ, 128), 0)
    head = lane < QH
    own_score = jnp.where(head, own[...], 0.0)
    best = own_score
    picks = [sel[0, 2 * p + s] for s in range(2) for p in range(NREP)]
    for c in range(64):
        best = jnp.where(row == picks[c], jnp.maximum(best, tops[c : c + 1]), best)
    total = jnp.exp(own_score - best)
    for c in range(64):
        added = jnp.exp(jnp.minimum(tops[c : c + 1] - best, 0.0)) * sums[c : c + 1]
        total = total + jnp.where(row == picks[c], added, 0.0)
    inverse = 1.0 / total
    own_factor = jnp.where(head, jnp.exp(own_score - best) * inverse, 0.0)
    factors[0:32, :] = best
    factors[32:64, :] = inverse
    lines = []
    for c in range(64):
        high = factors[pl.ds(picks[c], 1), :]
        scaled = factors[pl.ds(picks[c] + 32, 1), :]
        lines.append(jnp.exp(jnp.minimum(tops[c : c + 1] - high, 0.0)) * scaled)
    turned = jnp.concatenate(lines + [own_factor, jnp.zeros((32, 128), F32)], axis=0).T
    turned = turned[:QH, :]
    for i in range(REQ):
        values = jnp.concatenate(
            [
                jnp.broadcast_to(
                    new_kv[i : i + 1, (KVH + g) * HD : (KVH + g + 1) * HD].astype(F32), (8, HD)
                )
                for g in range(KVH)
            ],
            axis=0,
        )
        acc[i * QH : (i + 1) * QH, :] = turned[:, 64 + i : 65 + i] * values
    for c in range(64):
        s, p = c // 32, c % 32
        at = pl.ds(pl.multiple_of(picks[c] * QH, QH), QH)
        given = recv[p, s * QH : (s + 1) * QH, :].astype(F32)
        acc[at, :] = acc[at, :] + turned[:, c : c + 1] * given
    for h in range(QH):
        out[:, h * HD : (h + 1) * HD] = acc[pl.ds(h, REQ, stride=QH), :].astype(BF16)


def exchange(values, axis):
    return lax.all_to_all(values, axis, split_axis=0, concat_axis=0, tiled=True)


def shards(
    hidden,
    base_query_rows,
    new_kv,
    adapter_down_matrix,
    adapter_up_matrix,
    holder,
    adapter_slot,
    kv_pages,
    mig_pages,
    page_owner,
    page_used,
):
    owner = in_hbm(page_owner.reshape(1, POOL))
    outgoing, pos = call(
        dispatch_body,
        [pltpu.HBM((256, WIDE), BF16), shape((1, 128), I32)],
        scratch=[
            pltpu.VMEM((REQ, 4 * QUART), BF16),
            pltpu.VMEM((1, REQ), I32),
            pltpu.VMEM((1, REQ), I32),
            pltpu.VMEM((1, POOL), I32),
            pltpu.VMEM((256, WIDE), BF16),
            sems(8),
        ],
        ins=[ANY] * 4,
        out_specs=[ANY, VM],
        moved=2 << 20,
    )(in_hbm(hidden), in_hbm(holder.reshape(1, REQ)), in_hbm(adapter_slot.reshape(1, REQ)), owner)
    rows_in = exchange(outgoing.reshape(NREP, 8, WIDE), "replica")

    flat_pages = in_hbm(kv_pages.reshape(96 * PAGE, 1024))
    *leaving, up = call(
        leave_body,
        [pltpu.VMEM((64, 1024), BF16)] * NBUC
        + [pltpu.VMEM(adapter_up_matrix.shape, BF16)],
        scratch=[sems(33)],
        ins=[SM] + [ANY] * 3,
        moved=6 << 20,
    )(
        mig_pages.reshape(1, 32),
        flat_pages,
        in_hbm(adapter_up_matrix),
        pos,
    )
    arrived = [leaving[0]] + [
        lax.ppermute(leaving[k], "bucket", [(s, s ^ k) for s in range(NBUC)]) for k in range(1, NBUC)
    ]
    arrived = [in_hbm(one) for one in arrived]

    raised, sel = call(
        adapter_body,
        [pltpu.HBM((2048, 128), BF16), shape((1, 128), I32)],
        scratch=[
            pltpu.VMEM((2048, 128), F32),
            pltpu.VMEM((2048, 128), BF16),
            pltpu.VMEM(adapter_down_matrix.shape, BF16),
            sems(12),
        ],
        ins=[VM, ANY, VM] + [ANY] * NBUC,
        out_specs=[ANY, VM],
        flops=1 << 30,
        moved=8 << 20,
    )(in_vmem(rows_in.reshape(256, WIDE)), in_hbm(adapter_down_matrix), in_vmem(up), *arrived)
    returned = exchange(raised.reshape(NREP, 64, 128), "replica")
    rowid, spread, member, keys, values = call(
        prepare_body,
        [
            shape((1, 128), I32),
            pltpu.VMEM((8, POOL * PAGE), I32),
            pltpu.VMEM((POOL * PAGE, 128), BF16),
            pltpu.VMEM((BLOCKS * KVH * HD, 128), BF16),
            pltpu.HBM((POOL * PAGE, KVH * HD), BF16),
        ],
        scratch=[
            pltpu.VMEM((1, POOL), I32),
            pltpu.VMEM((1, POOL), I32),
            pltpu.VMEM((96 * PAGE, 1024), BF16),
            pltpu.VMEM((32 * PAGE, 1024), BF16),
            pltpu.VMEM((POOL * PAGE, KVH * HD), BF16),
            sems(12),
        ],
        ins=[ANY] * (4 + NBUC),
        out_specs=[VM] * 4 + [ANY],
        mib=12,
        moved=8 << 20,
    )(owner, in_hbm(page_used.reshape(1, POOL)), flat_pages, sel, *arrived)

    queries, asked = call(
        query_body,
        [pltpu.VMEM((REQ * QH, HD), BF16), pltpu.HBM((2048, 128), BF16)],
        scratch=[
            pltpu.VMEM((REQ, QH * HD), BF16),
            pltpu.VMEM((REQ * QH, HD), F32),
            pltpu.VMEM((2048, 128), BF16),
            sems(5),
        ],
        ins=[SM, SM, VM, ANY, ANY],
        out_specs=[VM, ANY],
    )(pos, sel, in_vmem(returned.reshape(2048, 128)), in_hbm(base_query_rows), rowid)
    recv = exchange(asked.reshape(NREP, 64, 128), "replica")
    own, fresh = call(
        own_body,
        [pltpu.VMEM((REQ, 128), F32), pltpu.VMEM(new_kv.shape, BF16)],
        scratch=[sems(1)],
        ins=[VM, ANY],
    )(in_vmem(queries), in_hbm(new_kv))

    (partial,) = call(
        attend_body,
        [pltpu.HBM((NREP, CROWS, 128), BF16)],
        scratch=[
            pltpu.VMEM((2048, 128), F32),
            pltpu.VMEM((QH, POOL * PAGE), F32),
            pltpu.VMEM((2048, 128), F32),
            pltpu.VMEM((128, 128), F32),
            pltpu.VMEM((256, 128), F32),
            pltpu.VMEM((NREP, CROWS, 128), BF16),
            pltpu.VMEM((POOL * PAGE, KVH * HD), BF16),
            sems(5),
        ],
        ins=[SM] + [VM] * 4 + [ANY],
        out_specs=[ANY],
        flops=1 << 29,
        moved=6 << 20,
    )(
        rowid,
        in_vmem(spread),
        in_vmem(member),
        in_vmem(recv.reshape(2048, 128)),
        in_vmem(keys),
        in_hbm(values),
    )
    parts = exchange(partial, "replica")

    return call(
        combine_body,
        [shape((REQ, QH * HD), BF16)],
        scratch=[
            pltpu.VMEM((REQ * QH, HD), F32),
            pltpu.VMEM((256, 128), F32),
            pltpu.VMEM((64, 128), F32),
        ],
        ins=[SM, VM, VM, VM],
    )(sel, in_vmem(parts), in_vmem(own), in_vmem(fresh))[0]


def solution(mesh):
    rows = P(("bucket", "replica"), None)
    flat = P(("bucket", "replica"))
    placed = (
        rows,
        rows,
        rows,
        P(None, ("bucket", "replica")),
        rows,
        rows,
        flat,
        P(("bucket", "replica"), None, None),
        flat,
        flat,
        flat,
    )
    return jax.shard_map(
        shards, mesh=mesh, in_specs=placed, out_specs=rows, check_vma=False
    )
```

```python
import jax
import jax.numpy as jnp
from jax import lax
from jax.experimental import pallas as pl
from jax.experimental.pallas import tpu as pltpu
from jax.sharding import PartitionSpec as P

QH = 32
KVH = 4
HD = 128
RANK = 64
PAGE = 16
REQ = 32
NREP = 32
NBUC = 8
POOL = 128
QUART = 2048
WIDE = QUART + 128
BLOCKS = 16
CROWS = 72
DHALF = 4096
SPLIT = 1
SCALE = HD ** -0.5
LOW = -3e38
NEG = -1e30
HIGH = lax.Precision.HIGHEST
F32 = jnp.float32
BF16 = jnp.bfloat16
I32 = jnp.int32
VM = pl.BlockSpec(memory_space=pltpu.VMEM)
ANY = pl.BlockSpec(memory_space=pl.ANY)
SM = pl.BlockSpec(memory_space=pltpu.SMEM)


def iota(shape, axis):
    return lax.broadcasted_iota(I32, shape, axis)


def dot(left, right, precision=None):
    return jnp.dot(left, right, preferred_element_type=F32, precision=precision)


def call(body, outs, scratch=(), ins=None, out_specs=None, mib=8, flops=1 << 20, moved=1 << 20):
    return pl.pallas_call(
        body,
        out_shape=tuple(outs),
        in_specs=ins,
        out_specs=tuple(out_specs or [VM] * len(outs)),
        scratch_shapes=list(scratch),
        compiler_params=pltpu.CompilerParams(vmem_limit_bytes=mib << 20),
        cost_estimate=pl.CostEstimate(flops=flops, bytes_accessed=moved, transcendentals=0),
    )


def in_hbm(values):
    return pltpu.with_memory_space_constraint(values, pltpu.HBM)


def in_vmem(values):
    return pltpu.with_memory_space_constraint(values, pltpu.VMEM)


def begin(source, target, sem):
    copy = pltpu.make_async_copy(source, target, sem)
    copy.start()
    return copy


def sems(count):
    return pltpu.SemaphoreType.DMA((count,))


def shape(dims, kind):
    return jax.ShapeDtypeStruct(dims, kind)


def dispatch_body(hidden_in, holder_in, slot_in, owner_in, out, pos, hidden, holder, slot, owner, made, sem):
    small = [
        begin(source, target, sem.at[n])
        for n, (source, target) in enumerate(
            ((holder_in, holder), (slot_in, slot), (owner_in, owner))
        )
    ]
    large = begin(hidden_in, hidden, sem.at[3])
    for copy in small:
        copy.wait()
    square = (REQ, REQ)
    col = jnp.sum(
        jnp.where(iota(square, 0) == iota(square, 1), holder[...], 0), axis=1, keepdims=True
    )
    col4 = jnp.concatenate([col] * 4, axis=0)
    square = (128, 128)
    target = jnp.sum(jnp.where(iota(square, 0) == iota(square, 1), col4, 0), axis=0, keepdims=True)
    earlier = (col == target) & (iota((REQ, 128), 0) < (iota((REQ, 128), 1) & 31))
    rank = jnp.sum(jnp.where(earlier, 1, 0), axis=0, keepdims=True)
    place = 2 * target + rank
    pos[...] = place
    full = (256, 128)
    row, lane = iota(full, 0), iota(full, 1)
    at_place = (row >> 2) == place
    onehot = jnp.where(at_place & ((row & 3) == (lane >> 5)), 1.0, 0.0).astype(BF16)
    slot_col = jnp.sum(jnp.where(at_place[:, :REQ], slot[...], 0), axis=1, keepdims=True)
    own = owner[...]
    here = (own >> 5) == (row >> 3)
    local = own & 31
    least = jnp.min(jnp.where(here, local, 99), axis=1, keepdims=True)
    most = jnp.max(jnp.where(here, local, -1), axis=1, keepdims=True)
    second = ((row >> 2) & 1) == 1
    chosen = jnp.where(second, most, least)
    meta = jnp.where(lane == 0, slot_col, jnp.where(lane == 1, chosen, 0))
    made[:, QUART:] = meta.astype(F32).astype(BF16)
    large.wait()
    stacked = jnp.concatenate([hidden[:, q * QUART : (q + 1) * QUART] for q in range(4)], axis=0)
    copies = []
    for n in range(4):
        rows = slice(n * 64, (n + 1) * 64)
        made[rows, :QUART] = dot(onehot[rows], stacked).astype(BF16)
        copies.append(begin(made.at[n * 64 : (n + 1) * 64], out.at[n * 64 : (n + 1) * 64], sem.at[4 + n]))
    for copy in copies:
        copy.wait()


def prepare_body(owner_in, used_in, pages_in, base_in, after, *rest):
    given, outs, scratch = rest[:NBUC], rest[NBUC : NBUC + 7], rest[NBUC + 7 :]
    rowid, spread, reqcol, based, keys, member, values_out = outs
    owner, used, pages, pieces, base, turned, values, sem = scratch
    copies = [
        begin(source, target, sem.at[n])
        for n, (source, target) in enumerate(
            ((owner_in, owner), (used_in, used), (base_in, base), (pages_in, pages))
        )
    ]
    arrived = [pieces.at[k * 64 : (k + 1) * 64] for k in range(NBUC)]
    copies += [begin(given[k], arrived[k], sem.at[4 + k]) for k in range(NBUC)]
    copies[0].wait()
    copies[1].wait()
    own = owner[...]
    square = (128, 128)
    row, lane = iota(square, 0), iota(square, 1)
    own_col = jnp.sum(jnp.where(row == lane, own, 0), axis=1, keepdims=True)
    least = jnp.min(jnp.where((own_col >> 5) == (own >> 5), own_col, 1 << 20), axis=0, keepdims=True)
    ids = 2 * (own >> 5) + jnp.where(own > least, 1, 0)
    both = jnp.where(
        iota((16, 128), 0) == 0, ids, jnp.where(iota((16, 128), 0) == 1, used[...], 0)
    ).astype(F32).astype(BF16)
    turn = lax.axis_index("bucket") << 2

    def moved(slot):
        return jnp.where(slot < 96, slot, slot ^ turn)

    one = jnp.where(row == moved(lane), 1.0, 0.0).astype(BF16)
    rowid[...] = dot(both, one)[:1].astype(I32)
    wide = (128, POOL * PAGE)
    onehot = jnp.where(iota(wide, 0) == moved(iota(wide, 1) >> 4), 1.0, 0.0).astype(BF16)
    spread[...] = dot(both, onehot)[:8].astype(I32)
    tall = (POOL * PAGE, 128)
    onehot = jnp.where(iota(tall, 1) == moved(iota(tall, 0) >> 4), 1.0, 0.0).astype(BF16)
    ids_col = jnp.sum(jnp.where(row == lane, ids, 0), axis=1, keepdims=True)
    member[...] = dot(onehot, jnp.where(ids_col == lane, 1.0, 0.0).astype(BF16)).astype(BF16)
    slot = ((row & 15) << 3) + (row >> 4)
    reqcol[...] = jnp.broadcast_to(
        jnp.sum(jnp.where(lane == moved(slot), ids, 0), axis=1, keepdims=True), square
    )
    copies[2].wait()
    for h in range(QH):
        turned[pl.ds(h, REQ, stride=QH), :] = base[:, h * HD : (h + 1) * HD].astype(F32)
    based[...] = turned[...].astype(BF16)
    for copy in copies[3:]:
        copy.wait()
    for b in range(12):
        rows = slice(b * 128, (b + 1) * 128)
        values[rows, :] = pages[rows, KVH * HD :]
    for k in range(NBUC):
        values[(24 + k) * 64 : (25 + k) * 64, :] = arrived[k][:, KVH * HD :]
    store = begin(values, values_out, sem.at[12])
    for b in range(BLOCKS):
        for g in range(KVH):
            cut = slice(g * HD, (g + 1) * HD)
            if b < 12:
                block = pages[b * 128 : (b + 1) * 128, cut]
            else:
                block = jnp.concatenate([one[:, cut] for one in arrived[2 * b - 24 : 2 * b - 22]], axis=0)
            keys[(b * KVH + g) * HD : (b * KVH + g + 1) * HD, :] = block.T
    store.wait()


def leave_body(mig, pages, down_in, after, *rest):
    outs, (down, sem) = rest[:NBUC], rest[NBUC:]
    me = lax.axis_index("bucket")
    copies = []
    for k in range(NBUC):
        for j in range(4):
            page = mig[0, (me ^ k) * 4 + j]
            copies.append(
                begin(
                    pages.at[pl.ds(pl.multiple_of(page * PAGE, PAGE), PAGE)],
                    outs[k].at[pl.ds(j * PAGE, PAGE)],
                    sem.at[k * 4 + j],
                )
            )
    copies.append(begin(down_in.at[:DHALF], down, sem.at[32]))
    for copy in copies:
        copy.wait()


def adapter_body(rows, early, down_in, up_in, *rest):
    raised, sel, spare, packed, down, up, sem = rest[NBUC:]
    loads = [
        begin(down_in.at[DHALF + n * 1024 : DHALF + (n + 1) * 1024], down.at[n * 1024 : (n + 1) * 1024], sem.at[4 + n])
        for n in range(4)
    ]
    load_up = begin(up_in, up, sem.at[8])
    part = iota((256, 256), 0) & 3
    total = jnp.zeros((256, 256), F32)
    for q in range(4):
        if q < 2:
            weights = early[q * QUART : (q + 1) * QUART, :]
        else:
            loads[2 * q - 4].wait()
            loads[2 * q - 3].wait()
            weights = down[(q - 2) * QUART : (q - 1) * QUART, :]
        total = total + jnp.where(part == q, dot(rows[:, :QUART], weights), 0.0)
    for k in range(2):
        spare[k * 256 : (k + 1) * 256, :] = total[:, k * 128 : (k + 1) * 128]
    lowered = jnp.concatenate(
        [
            sum(spare[pl.ds(k * 256 + q, 64, stride=4), :] for q in range(4))
            for k in range(2)
        ],
        axis=1,
    )
    first = jnp.where(iota((64, 256), 1) == 4 * iota((64, 256), 0), 1.0, 0.0).astype(BF16)
    meta = dot(first, rows[:, QUART:]).astype(I32)
    sel[...] = jnp.sum(
        jnp.where(iota((64, 128), 0) == iota((64, 128), 1), meta[:, 1:2], 0), axis=0, keepdims=True
    )
    chosen = meta[:, 0:1] == (iota((64, 256), 1) >> 6)
    kept = jnp.where(chosen, lowered, 0.0).astype(BF16)
    load_up.wait()
    for n in range(16):
        piece = dot(kept, up[:, n * 256 : (n + 1) * 256])
        spare[pl.ds(2 * n, 64, stride=32), :] = piece[:, :128]
        spare[pl.ds(2 * n + 1, 64, stride=32), :] = piece[:, 128:]
    copies = []
    for n in range(4):
        packed[n * 512 : (n + 1) * 512, :] = spare[n * 512 : (n + 1) * 512, :].astype(BF16)
        copies.append(
            begin(packed.at[n * 512 : (n + 1) * 512], raised.at[n * 512 : (n + 1) * 512], sem.at[n])
        )
    for copy in copies:
        copy.wait()


def query_body(pos, sel, delta, based, queries, out, packed, sem):
    for i in range(REQ):
        from_row = pl.multiple_of(pos[0, i] * QH, QH)
        rows = slice(i * QH, (i + 1) * QH)
        queries[rows, :] = (based[rows, :].astype(F32) + delta[pl.ds(from_row, QH), :].astype(F32)).astype(BF16)
    copies = []
    for c in range(2 * NREP):
        from_row = pl.multiple_of(sel[0, c] * QH, QH)
        packed[c * QH : (c + 1) * QH, :] = queries[pl.ds(from_row, QH), :]
        if c % 16 == 15:
            n = c // 16
            copies.append(
                begin(packed.at[n * 512 : (n + 1) * 512], out.at[n * 512 : (n + 1) * 512], sem.at[n])
            )
    for copy in copies:
        copy.wait()


def own_body(queries, new_in, own, new_kv, sem):
    begin(new_in, new_kv, sem.at[0]).wait()
    lane = iota((QH, 128), 1)
    columns = jnp.zeros((QH, 128), F32)
    for i in range(REQ):
        query = queries[i * QH : (i + 1) * QH, :].astype(F32)
        keys = jnp.concatenate(
            [
                jnp.broadcast_to(new_kv[i : i + 1, g * HD : (g + 1) * HD].astype(F32), (8, HD))
                for g in range(KVH)
            ],
            axis=0,
        )
        columns = jnp.where(lane == i, jnp.sum(query * keys, axis=1, keepdims=True), columns)
    padded = jnp.concatenate([columns, jnp.zeros((96, 128), F32)], axis=0)
    own[...] = padded.T[:REQ, :] * SCALE


def merge_pages(blocks):
    lane = iota((QH, 128), 1)
    for step in (8, 4, 2, 1):
        upper = (lane & step) != 0
        merged = []
        for first, second in zip(blocks[:step], blocks[step:]):
            stay = jnp.where(upper, second, first)
            swap = jnp.where(upper, first, second)
            swap = jnp.where(upper, pltpu.roll(swap, step, 1), pltpu.roll(swap, 128 - step, 1))
            merged.append(jnp.maximum(stay, swap))
        blocks = merged
    return blocks[0]


def split3(values):
    high = values.astype(BF16).astype(F32)
    rest = values - high
    middle = rest.astype(BF16).astype(F32)
    return high, middle, rest - middle


def attend_body(
    rowid, spread, reqcol, recv, keys, member, values_in, out,
    qf, cs, spare, stats, packed, values, sem, *accs,
):
    load_values = begin(values_in, values, sem.at[4])
    qf[...] = recv[...].astype(F32)
    for acc in accs:
        acc[...] = jnp.zeros_like(acc)
    page8 = iota((8, 128), 1) >> 4
    ids = [rowid[0, p] * QH for p in range(POOL)]
    for b in range(BLOCKS):
        cut = slice(b * 128, (b + 1) * 128)
        for g in range(KVH):
            query = jnp.concatenate(
                [qf[pl.ds(pl.multiple_of(ids[b * 8 + i] + g * 8, 8), 8), :] for i in range(8)], axis=0
            ).astype(BF16)
            found = dot(query, keys[(b * KVH + g) * HD : (b * KVH + g + 1) * HD, :])
            kept = found[0:8]
            for i in range(1, 8):
                kept = jnp.where(page8 == i, found[i * 8 : (i + 1) * 8], kept)
            cs[g * 8 : (g + 1) * 8, cut] = kept

    spot = iota((QH, 128), 1) & 15
    valid, blocks = [], []
    for b in range(BLOCKS):
        cut = slice(b * 128, (b + 1) * 128)
        valid.append(spot < spread[1:2, cut])
        blocks.append(jnp.where(valid[b], cs[:, cut] * SCALE, NEG))
        cs[:, cut] = blocks[b]
    merged = merge_pages(blocks)
    turned = jnp.concatenate([merged] * 4, axis=0).T
    which = reqcol[...] - (iota((128, 128), 1) >> 5)
    tops = jnp.full((128, 128), LOW, F32)
    lines = []
    for n in range(16):
        mine = which == 4 * n
        top = jnp.max(jnp.where(mine, turned, LOW), axis=0, keepdims=True)
        lines.append(top)
        tops = jnp.where(mine, top, tops)
    tops = jnp.maximum(tops, pltpu.roll(tops, 32, 1))
    tops = jnp.maximum(tops, pltpu.roll(tops, 64, 1)).T[:QH, :]
    pieces = jnp.concatenate(split3(tops), axis=0).astype(BF16)
    place = iota((128, 128), 0) - ((iota((128, 128), 1) >> 4) << 4)
    sums = jnp.zeros((QH, 128), F32)
    for b in range(BLOCKS):
        cut = slice(b * 128, (b + 1) * 128)
        spread_tops = dot(pieces, jnp.where(place == b, 1.0, 0.0).astype(BF16))
        top = spread_tops[0:32] + spread_tops[32:64] + spread_tops[64:96]
        weight = jnp.where(valid[b], jnp.exp(cs[:, cut] - top), 0.0).astype(BF16)
        cs[:, cut] = weight.astype(F32)
        sums = sums + dot(weight, member[cut, :])

    load_values.wait()
    for b in range(BLOCKS):
        cut = slice(b * 128, (b + 1) * 128)
        for g in range(KVH):
            weight = cs[g * 8 : (g + 1) * 8, cut]
            spread_weight = jnp.concatenate(
                [jnp.where(page8 == i, weight, 0.0) for i in range(8)], axis=0
            ).astype(BF16)
            found = dot(spread_weight, values[cut, g * HD : (g + 1) * HD])
            for i in range(8):
                at = pl.ds(pl.multiple_of(ids[b * 8 + i] // 4, 8), 8)
                acc = accs[(i % SPLIT) * KVH + g]
                acc[at, :] = acc[at, :] + found[i * 8 : (i + 1) * 8]

    stats[...] = jnp.zeros_like(stats)
    for n, piece in enumerate(split3(jnp.concatenate(lines, axis=0))):
        stats[pl.ds(n, 16, stride=16), :] = piece
        stats[pl.ds(8 + n, 16, stride=16), :] = pltpu.roll(piece, 64, 1)
    spare[...] = jnp.concatenate([sums, jnp.zeros((96, 128), F32)], axis=0).T
    line = spare[pl.ds(0, 32, stride=2), :] + pltpu.roll(spare[pl.ds(1, 32, stride=2), :], 32, 1)
    for n, piece in enumerate(split3(line)):
        stats[pl.ds(3 + n, 32, stride=8), :] = piece
    packed[:, 64:72, :] = stats[...].astype(BF16).reshape(NREP, 8, 128)
    copies = []
    for n in range(4):
        rows = slice(n * 128, (n + 1) * 128)
        groups = [
            sum(accs[k * KVH + g][rows, :] for k in range(SPLIT)).reshape(16, 8, HD)
            for g in range(KVH)
        ]
        part = jnp.concatenate(groups, axis=1).reshape(8, 64, HD)
        packed[n * 8 : (n + 1) * 8, 0:64, :] = part.astype(BF16)
        copies.append(
            begin(packed.at[n * 8 : (n + 1) * 8], out.at[n * 8 : (n + 1) * 8], sem.at[n])
        )
    for copy in copies:
        copy.wait()


def combine_body(sel, recv, own, new_kv, out, acc, stats, factors):
    stats[...] = recv[:, 64:72, :].astype(F32).reshape(NREP * 8, 128)

    def stat(k):
        read = [stats[pl.ds(3 * k + n, 32, stride=8), :] for n in range(3)]
        return read[0] + read[1] + read[2]

    tops, sums = stat(0), stat(1)
    tops = jnp.concatenate([tops, pltpu.roll(tops, 96, 1)], axis=0)
    sums = jnp.concatenate([sums, pltpu.roll(sums, 96, 1)], axis=0)
    lane = iota((REQ, 128), 1)
    row = iota((REQ, 128), 0)
    head = lane < QH
    own_score = jnp.where(head, own[...], 0.0)
    best = own_score
    picks = [sel[0, 2 * p + s] for s in range(2) for p in range(NREP)]
    for c in range(64):
        best = jnp.where(row == picks[c], jnp.maximum(best, tops[c : c + 1]), best)
    total = jnp.exp(own_score - best)
    for c in range(64):
        added = jnp.exp(jnp.minimum(tops[c : c + 1] - best, 0.0)) * sums[c : c + 1]
        total = total + jnp.where(row == picks[c], added, 0.0)
    inverse = 1.0 / total
    own_factor = jnp.where(head, jnp.exp(own_score - best) * inverse, 0.0)
    factors[0:32, :] = best
    factors[32:64, :] = inverse
    lines = []
    for c in range(64):
        high = factors[pl.ds(picks[c], 1), :]
        scaled = factors[pl.ds(picks[c] + 32, 1), :]
        lines.append(jnp.exp(jnp.minimum(tops[c : c + 1] - high, 0.0)) * scaled)
    turned = jnp.concatenate(lines + [own_factor, jnp.zeros((32, 128), F32)], axis=0).T
    turned = turned[:QH, :]
    for i in range(REQ):
        values = jnp.concatenate(
            [
                jnp.broadcast_to(
                    new_kv[i : i + 1, (KVH + g) * HD : (KVH + g + 1) * HD].astype(F32), (8, HD)
                )
                for g in range(KVH)
            ],
            axis=0,
        )
        acc[i * QH : (i + 1) * QH, :] = turned[:, 64 + i : 65 + i] * values
    for c in range(64):
        s, p = c // 32, c % 32
        at = pl.ds(pl.multiple_of(picks[c] * QH, QH), QH)
        given = recv[p, s * QH : (s + 1) * QH, :].astype(F32)
        acc[at, :] = acc[at, :] + turned[:, c : c + 1] * given
    for h in range(QH):
        out[:, h * HD : (h + 1) * HD] = acc[pl.ds(h, REQ, stride=QH), :].astype(BF16)


def exchange(values, axis):
    return lax.all_to_all(values, axis, split_axis=0, concat_axis=0, tiled=True)


def shards(
    hidden,
    base_query_rows,
    new_kv,
    adapter_down_matrix,
    adapter_up_matrix,
    holder,
    adapter_slot,
    kv_pages,
    mig_pages,
    page_owner,
    page_used,
):
    owner = in_hbm(page_owner.reshape(1, POOL))
    outgoing, pos = call(
        dispatch_body,
        [pltpu.HBM((256, WIDE), BF16), shape((1, 128), I32)],
        scratch=[
            pltpu.VMEM((REQ, 4 * QUART), BF16),
            pltpu.VMEM((1, REQ), I32),
            pltpu.VMEM((1, REQ), I32),
            pltpu.VMEM((1, POOL), I32),
            pltpu.VMEM((256, WIDE), BF16),
            sems(8),
        ],
        ins=[ANY] * 4,
        out_specs=[ANY, VM],
        moved=2 << 20,
    )(in_hbm(hidden), in_hbm(holder.reshape(1, REQ)), in_hbm(adapter_slot.reshape(1, REQ)), owner)
    rows_in = exchange(outgoing.reshape(NREP, 8, WIDE), "replica")

    down = in_hbm(adapter_down_matrix)
    flat_pages = in_hbm(kv_pages.reshape(96 * PAGE, 1024))
    *leaving, early = call(
        leave_body,
        [pltpu.VMEM((64, 1024), BF16)] * NBUC
        + [pltpu.VMEM((DHALF, 256), BF16)],
        scratch=[sems(33)],
        ins=[SM] + [ANY] * 3,
        moved=6 << 20,
    )(
        mig_pages.reshape(1, 32),
        flat_pages,
        down,
        pos,
    )
    arrived = [leaving[0]] + [
        lax.ppermute(leaving[k], "bucket", [(s, s ^ k) for s in range(NBUC)]) for k in range(1, NBUC)
    ]
    arrived = [in_hbm(one) for one in arrived]

    raised, sel = call(
        adapter_body,
        [pltpu.HBM((2048, 128), BF16), shape((1, 128), I32)],
        scratch=[
            pltpu.VMEM((2048, 128), F32),
            pltpu.VMEM((2048, 128), BF16),
            pltpu.VMEM((DHALF, 256), BF16),
            pltpu.VMEM(adapter_up_matrix.shape, BF16),
            sems(9),
        ],
        ins=[VM, VM] + [ANY] * (2 + NBUC),
        out_specs=[ANY, VM],
        flops=1 << 30,
        moved=8 << 20,
    )(
        in_vmem(rows_in.reshape(256, WIDE)),
        in_vmem(early),
        down,
        in_hbm(adapter_up_matrix),
        *arrived,
    )
    returned = exchange(raised.reshape(NREP, 64, 128), "replica")
    rowid, spread, reqcol, based, keys, member, values = call(
        prepare_body,
        [
            shape((1, 128), I32),
            pltpu.VMEM((8, POOL * PAGE), I32),
            pltpu.VMEM((128, 128), I32),
            pltpu.VMEM((REQ * QH, HD), BF16),
            pltpu.VMEM((BLOCKS * KVH * HD, 128), BF16),
            pltpu.VMEM((POOL * PAGE, 128), BF16),
            pltpu.HBM((POOL * PAGE, KVH * HD), BF16),
        ],
        scratch=[
            pltpu.VMEM((1, POOL), I32),
            pltpu.VMEM((1, POOL), I32),
            pltpu.VMEM((96 * PAGE, 1024), BF16),
            pltpu.VMEM((32 * PAGE, 1024), BF16),
            pltpu.VMEM((REQ, QH * HD), BF16),
            pltpu.VMEM((REQ * QH, HD), F32),
            pltpu.VMEM((POOL * PAGE, KVH * HD), BF16),
            sems(13),
        ],
        ins=[ANY] * (5 + NBUC),
        out_specs=[VM] * 6 + [ANY],
        mib=14,
        moved=8 << 20,
    )(
        owner,
        in_hbm(page_used.reshape(1, POOL)),
        flat_pages,
        in_hbm(base_query_rows),
        sel,
        *arrived,
    )

    queries, asked = call(
        query_body,
        [pltpu.VMEM((REQ * QH, HD), BF16), pltpu.HBM((2048, 128), BF16)],
        scratch=[pltpu.VMEM((2048, 128), BF16), sems(4)],
        ins=[SM, SM, VM, VM],
        out_specs=[VM, ANY],
    )(pos, sel, in_vmem(returned.reshape(2048, 128)), in_vmem(based))
    recv = exchange(asked.reshape(NREP, 64, 128), "replica")
    own, fresh = call(
        own_body,
        [pltpu.VMEM((REQ, 128), F32), pltpu.VMEM(new_kv.shape, BF16)],
        scratch=[sems(1)],
        ins=[VM, ANY],
    )(in_vmem(queries), in_hbm(new_kv))

    (partial,) = call(
        attend_body,
        [pltpu.HBM((NREP, CROWS, 128), BF16)],
        scratch=[
            pltpu.VMEM((2048, 128), F32),
            pltpu.VMEM((QH, POOL * PAGE), F32),
            pltpu.VMEM((128, 128), F32),
            pltpu.VMEM((256, 128), F32),
            pltpu.VMEM((NREP, CROWS, 128), BF16),
            pltpu.VMEM((POOL * PAGE, KVH * HD), BF16),
            sems(5),
        ]
        + [pltpu.VMEM((512, 128), F32)] * (SPLIT * KVH),
        ins=[SM] + [VM] * 5 + [ANY],
        out_specs=[ANY],
        mib=12,
        flops=1 << 29,
        moved=6 << 20,
    )(
        rowid,
        in_vmem(spread),
        in_vmem(reqcol),
        in_vmem(recv.reshape(2048, 128)),
        in_vmem(keys),
        in_vmem(member),
        in_hbm(values),
    )
    parts = exchange(partial, "replica")

    return call(
        combine_body,
        [shape((REQ, QH * HD), BF16)],
        scratch=[
            pltpu.VMEM((REQ * QH, HD), F32),
            pltpu.VMEM((256, 128), F32),
            pltpu.VMEM((64, 128), F32),
        ],
        ins=[SM, VM, VM, VM],
    )(sel, in_vmem(parts), in_vmem(own), in_vmem(fresh))[0]


def solution(mesh):
    rows = P(("bucket", "replica"), None)
    flat = P(("bucket", "replica"))
    placed = (
        rows,
        rows,
        rows,
        P(None, ("bucket", "replica")),
        rows,
        rows,
        flat,
        P(("bucket", "replica"), None, None),
        flat,
        flat,
        flat,
    )
    return jax.shard_map(
        shards, mesh=mesh, in_specs=placed, out_specs=rows, check_vma=False
    )
```

```python
import jax
import jax.numpy as jnp
from jax import lax
from jax.experimental import pallas as pl
from jax.experimental.pallas import tpu as pltpu
from jax.sharding import PartitionSpec as P

QH = 32
KVH = 4
HD = 128
RANK = 64
PAGE = 16
REQ = 32
NREP = 32
NBUC = 8
POOL = 128
QUART = 2048
WIDE = QUART + 128
BLOCKS = 16
CROWS = 72
DHALF = 4096
SPLIT = 1
SCALE = HD ** -0.5
LOW = -3e38
NEG = -1e30
HIGH = lax.Precision.HIGHEST
F32 = jnp.float32
BF16 = jnp.bfloat16
I32 = jnp.int32
VM = pl.BlockSpec(memory_space=pltpu.VMEM)
ANY = pl.BlockSpec(memory_space=pl.ANY)
SM = pl.BlockSpec(memory_space=pltpu.SMEM)


def iota(shape, axis):
    return lax.broadcasted_iota(I32, shape, axis)


def dot(left, right, precision=None):
    return jnp.dot(left, right, preferred_element_type=F32, precision=precision)


def call(body, outs, scratch=(), ins=None, out_specs=None, mib=24, flops=1 << 20, moved=1 << 20):
    return pl.pallas_call(
        body,
        out_shape=tuple(outs),
        in_specs=ins,
        out_specs=tuple(out_specs or [VM] * len(outs)),
        scratch_shapes=list(scratch),
        compiler_params=pltpu.CompilerParams(vmem_limit_bytes=mib << 20),
        cost_estimate=pl.CostEstimate(flops=flops, bytes_accessed=moved, transcendentals=0),
    )


def in_hbm(values):
    return pltpu.with_memory_space_constraint(values, pltpu.HBM)


def in_vmem(values):
    return pltpu.with_memory_space_constraint(values, pltpu.VMEM)


def begin(source, target, sem):
    copy = pltpu.make_async_copy(source, target, sem)
    copy.start()
    return copy


def sems(count):
    return pltpu.SemaphoreType.DMA((count,))


def shape(dims, kind):
    return jax.ShapeDtypeStruct(dims, kind)


def dispatch_body(hidden_in, holder_in, slot_in, owner_in, out, pos, hidden, holder, slot, owner, made, sem):
    small = [
        begin(source, target, sem.at[n])
        for n, (source, target) in enumerate(
            ((holder_in, holder), (slot_in, slot), (owner_in, owner))
        )
    ]
    large = begin(hidden_in, hidden, sem.at[3])
    for copy in small:
        copy.wait()
    square = (REQ, REQ)
    col = jnp.sum(
        jnp.where(iota(square, 0) == iota(square, 1), holder[...], 0), axis=1, keepdims=True
    )
    col4 = jnp.concatenate([col] * 4, axis=0)
    square = (128, 128)
    target = jnp.sum(jnp.where(iota(square, 0) == iota(square, 1), col4, 0), axis=0, keepdims=True)
    earlier = (col == target) & (iota((REQ, 128), 0) < (iota((REQ, 128), 1) & 31))
    rank = jnp.sum(jnp.where(earlier, 1, 0), axis=0, keepdims=True)
    place = 2 * target + rank
    pos[...] = place
    full = (256, 128)
    row, lane = iota(full, 0), iota(full, 1)
    at_place = (row >> 2) == place
    onehot = jnp.where(at_place & ((row & 3) == (lane >> 5)), 1.0, 0.0).astype(BF16)
    slot_col = jnp.sum(jnp.where(at_place[:, :REQ], slot[...], 0), axis=1, keepdims=True)
    own = owner[...]
    here = (own >> 5) == (row >> 3)
    local = own & 31
    least = jnp.min(jnp.where(here, local, 99), axis=1, keepdims=True)
    most = jnp.max(jnp.where(here, local, -1), axis=1, keepdims=True)
    second = ((row >> 2) & 1) == 1
    chosen = jnp.where(second, most, least)
    meta = jnp.where(lane == 0, slot_col, jnp.where(lane == 1, chosen, 0))
    made[:, QUART:] = meta.astype(F32).astype(BF16)
    large.wait()
    stacked = jnp.concatenate([hidden[:, q * QUART : (q + 1) * QUART] for q in range(4)], axis=0)
    copies = []
    for n in range(4):
        rows = slice(n * 64, (n + 1) * 64)
        made[rows, :QUART] = dot(onehot[rows], stacked).astype(BF16)
        copies.append(begin(made.at[n * 64 : (n + 1) * 64], out.at[n * 64 : (n + 1) * 64], sem.at[4 + n]))
    for copy in copies:
        copy.wait()


def prepare_body(owner_in, used_in, pages_in, base_in, after, *rest):
    given, outs, scratch = rest[:NBUC], rest[NBUC : NBUC + 6], rest[NBUC + 6 :]
    rowid, spread, reqcol, based, keys, values_out = outs
    owner, used, pages, pieces, base, turned, values, sem = scratch
    copies = [
        begin(source, target, sem.at[n])
        for n, (source, target) in enumerate(
            ((owner_in, owner), (used_in, used), (base_in, base), (pages_in, pages))
        )
    ]
    arrived = [pieces.at[k * 64 : (k + 1) * 64] for k in range(NBUC)]
    copies += [begin(given[k], arrived[k], sem.at[4 + k]) for k in range(NBUC)]
    copies[0].wait()
    copies[1].wait()
    own = owner[...]
    square = (128, 128)
    row, lane = iota(square, 0), iota(square, 1)
    own_col = jnp.sum(jnp.where(row == lane, own, 0), axis=1, keepdims=True)
    least = jnp.min(jnp.where((own_col >> 5) == (own >> 5), own_col, 1 << 20), axis=0, keepdims=True)
    ids = 2 * (own >> 5) + jnp.where(own > least, 1, 0)
    both = jnp.where(
        iota((16, 128), 0) == 0, ids, jnp.where(iota((16, 128), 0) == 1, used[...], 0)
    ).astype(F32).astype(BF16)
    turn = lax.axis_index("bucket") << 2

    def moved(slot):
        return jnp.where(slot < 96, slot, slot ^ turn)

    one = jnp.where(row == moved(lane), 1.0, 0.0).astype(BF16)
    rowid[...] = dot(both, one)[:1].astype(I32)
    wide = (128, POOL * PAGE)
    onehot = jnp.where(iota(wide, 0) == moved(iota(wide, 1) >> 4), 1.0, 0.0).astype(BF16)
    spread[...] = dot(both, onehot)[:8].astype(I32)
    slot = ((row & 15) << 3) + (row >> 4)
    reqcol[...] = jnp.broadcast_to(
        jnp.sum(jnp.where(lane == moved(slot), ids, 0), axis=1, keepdims=True), square
    )
    copies[2].wait()
    for h in range(QH):
        turned[pl.ds(h, REQ, stride=QH), :] = base[:, h * HD : (h + 1) * HD].astype(F32)
    based[...] = turned[...].astype(BF16)
    for copy in copies[3:]:
        copy.wait()
    for b in range(12):
        rows = slice(b * 128, (b + 1) * 128)
        values[rows, :] = pages[rows, KVH * HD :]
    for k in range(NBUC):
        values[(24 + k) * 64 : (25 + k) * 64, :] = arrived[k][:, KVH * HD :]
    store = begin(values, values_out, sem.at[12])
    for b in range(BLOCKS):
        for g in range(KVH):
            cut = slice(g * HD, (g + 1) * HD)
            if b < 12:
                block = pages[b * 128 : (b + 1) * 128, cut]
            else:
                block = jnp.concatenate([one[:, cut] for one in arrived[2 * b - 24 : 2 * b - 22]], axis=0)
            keys[(b * KVH + g) * HD : (b * KVH + g + 1) * HD, :] = block.T
    store.wait()


def leave_body(mig, pages, down_in, after, *rest):
    outs, (down, sem) = rest[:NBUC], rest[NBUC:]
    me = lax.axis_index("bucket")
    copies = []
    for k in range(NBUC):
        for j in range(4):
            page = mig[0, (me ^ k) * 4 + j]
            copies.append(
                begin(
                    pages.at[pl.ds(pl.multiple_of(page * PAGE, PAGE), PAGE)],
                    outs[k].at[pl.ds(j * PAGE, PAGE)],
                    sem.at[k * 4 + j],
                )
            )
    copies.append(begin(down_in.at[:DHALF], down, sem.at[32]))
    for copy in copies:
        copy.wait()


def adapter_body(rows, early, down_in, up_in, *rest):
    raised, sel, spare, packed, down, up, apart, sem = rest[NBUC:]
    loads = [
        begin(down_in.at[DHALF + n * 1024 : DHALF + (n + 1) * 1024], down.at[n * 1024 : (n + 1) * 1024], sem.at[4 + n])
        for n in range(4)
    ]
    load_up = begin(up_in, up, sem.at[8])
    lowered = jnp.zeros((64, 256), F32)
    for n in range(QUART // 128):
        apart[n * 256 : (n + 1) * 256, :] = rows[:, n * 128 : (n + 1) * 128].astype(F32)
    for q in range(4):
        data = jnp.concatenate(
            [apart[pl.ds(n * 256 + q, 64, stride=4), :] for n in range(QUART // 128)], axis=1
        ).astype(BF16)
        if q < 2:
            weights = early[q * QUART : (q + 1) * QUART, :]
        else:
            loads[2 * q - 4].wait()
            loads[2 * q - 3].wait()
            weights = down[(q - 2) * QUART : (q - 1) * QUART, :]
        lowered = lowered + dot(data, weights)
    first = jnp.where(iota((64, 256), 1) == 4 * iota((64, 256), 0), 1.0, 0.0).astype(BF16)
    meta = dot(first, rows[:, QUART:]).astype(I32)
    sel[...] = jnp.sum(
        jnp.where(iota((64, 128), 0) == iota((64, 128), 1), meta[:, 1:2], 0), axis=0, keepdims=True
    )
    chosen = meta[:, 0:1] == (iota((64, 256), 1) >> 6)
    kept = jnp.where(chosen, lowered, 0.0).astype(BF16)
    load_up.wait()
    for n in range(16):
        piece = dot(kept, up[:, n * 256 : (n + 1) * 256])
        spare[pl.ds(2 * n, 64, stride=32), :] = piece[:, :128]
        spare[pl.ds(2 * n + 1, 64, stride=32), :] = piece[:, 128:]
    copies = []
    for n in range(4):
        packed[n * 512 : (n + 1) * 512, :] = spare[n * 512 : (n + 1) * 512, :].astype(BF16)
        copies.append(
            begin(packed.at[n * 512 : (n + 1) * 512], raised.at[n * 512 : (n + 1) * 512], sem.at[n])
        )
    for copy in copies:
        copy.wait()


def query_body(pos, sel, delta, based, queries, out, packed, sem):
    for i in range(REQ):
        from_row = pl.multiple_of(pos[0, i] * QH, QH)
        rows = slice(i * QH, (i + 1) * QH)
        queries[rows, :] = (based[rows, :].astype(F32) + delta[pl.ds(from_row, QH), :].astype(F32)).astype(BF16)
    copies = []
    for c in range(2 * NREP):
        from_row = pl.multiple_of(sel[0, c] * QH, QH)
        packed[c * QH : (c + 1) * QH, :] = queries[pl.ds(from_row, QH), :]
        if c % 16 == 15:
            n = c // 16
            copies.append(
                begin(packed.at[n * 512 : (n + 1) * 512], out.at[n * 512 : (n + 1) * 512], sem.at[n])
            )
    for copy in copies:
        copy.wait()


def fresh_body(new_in, after, fresh, sem):
    begin(new_in, fresh, sem.at[0]).wait()


def own_body(queries, new_in, own, new_kv, sem):
    begin(new_in, new_kv, sem.at[0]).wait()
    lane = iota((QH, 128), 1)
    columns = jnp.zeros((QH, 128), F32)
    for i in range(REQ):
        query = queries[i * QH : (i + 1) * QH, :].astype(F32)
        keys = jnp.concatenate(
            [
                jnp.broadcast_to(new_kv[i : i + 1, g * HD : (g + 1) * HD].astype(F32), (8, HD))
                for g in range(KVH)
            ],
            axis=0,
        )
        columns = jnp.where(lane == i, jnp.sum(query * keys, axis=1, keepdims=True), columns)
    padded = jnp.concatenate([columns, jnp.zeros((96, 128), F32)], axis=0)
    own[...] = padded.T[:REQ, :] * SCALE


def merge_pages(blocks):
    lane = iota((QH, 128), 1)
    for step in (8, 4, 2, 1):
        upper = (lane & step) != 0
        merged = []
        for first, second in zip(blocks[:step], blocks[step:]):
            stay = jnp.where(upper, second, first)
            swap = jnp.where(upper, first, second)
            swap = jnp.where(upper, pltpu.roll(swap, step, 1), pltpu.roll(swap, 128 - step, 1))
            merged.append(jnp.maximum(stay, swap))
        blocks = merged
    return blocks[0]


def split3(values):
    high = values.astype(BF16).astype(F32)
    rest = values - high
    middle = rest.astype(BF16).astype(F32)
    return high, middle, rest - middle


def attend_body(
    rowid, spread, reqcol, recv, keys, after, values_in, out,
    qf, cs, spare, stats, packed, values, sem, *accs,
):
    load_values = begin(values_in, values, sem.at[4])
    qf[...] = recv[...].astype(F32)
    for acc in accs:
        acc[...] = jnp.zeros_like(acc)
    page8 = iota((8, 128), 1) >> 4
    ids = [rowid[0, p] * QH for p in range(POOL)]
    for b in range(BLOCKS):
        cut = slice(b * 128, (b + 1) * 128)
        for g in range(KVH):
            query = jnp.concatenate(
                [qf[pl.ds(pl.multiple_of(ids[b * 8 + i] + g * 8, 8), 8), :] for i in range(8)], axis=0
            ).astype(BF16)
            found = dot(query, keys[(b * KVH + g) * HD : (b * KVH + g + 1) * HD, :])
            kept = found[0:8]
            for i in range(1, 8):
                kept = jnp.where(page8 == i, found[i * 8 : (i + 1) * 8], kept)
            cs[g * 8 : (g + 1) * 8, cut] = kept

    spot = iota((QH, 128), 1) & 15
    valid, blocks = [], []
    for b in range(BLOCKS):
        cut = slice(b * 128, (b + 1) * 128)
        valid.append(spot < spread[1:2, cut])
        blocks.append(jnp.where(valid[b], cs[:, cut] * SCALE, NEG))
        cs[:, cut] = blocks[b]
    merged = merge_pages(blocks)
    turned = jnp.concatenate([merged] * 4, axis=0).T
    which = reqcol[...] - (iota((128, 128), 1) >> 5)
    tops = jnp.full((128, 128), LOW, F32)
    lines = []
    for n in range(16):
        mine = which == 4 * n
        top = jnp.max(jnp.where(mine, turned, LOW), axis=0, keepdims=True)
        lines.append(top)
        tops = jnp.where(mine, top, tops)
    tops = jnp.maximum(tops, pltpu.roll(tops, 32, 1))
    tops = jnp.maximum(tops, pltpu.roll(tops, 64, 1)).T[:QH, :]
    pieces = jnp.concatenate(split3(tops), axis=0).astype(BF16)
    place = iota((128, 128), 0) - ((iota((128, 128), 1) >> 4) << 4)
    placed = iota((128, 128), 1) - ((iota((128, 128), 0) >> 4) << 4)
    sums = jnp.zeros((QH, 128), F32)
    for b in range(BLOCKS):
        cut = slice(b * 128, (b + 1) * 128)
        spread_tops = dot(pieces, jnp.where(place == b, 1.0, 0.0).astype(BF16))
        top = spread_tops[0:32] + spread_tops[32:64] + spread_tops[64:96]
        weight = jnp.where(valid[b], jnp.exp(cs[:, cut] - top), 0.0).astype(BF16)
        cs[:, cut] = weight.astype(F32)
        sums = sums + dot(weight, jnp.where(placed == b, 1.0, 0.0).astype(BF16))

    load_values.wait()
    for b in range(BLOCKS):
        cut = slice(b * 128, (b + 1) * 128)
        for g in range(KVH):
            weight = cs[g * 8 : (g + 1) * 8, cut]
            spread_weight = jnp.concatenate(
                [jnp.where(page8 == i, weight, 0.0) for i in range(8)], axis=0
            ).astype(BF16)
            found = dot(spread_weight, values[cut, g * HD : (g + 1) * HD])
            for i in range(8):
                at = pl.ds(pl.multiple_of(ids[b * 8 + i] // 4, 8), 8)
                acc = accs[(i % SPLIT) * KVH + g]
                acc[at, :] = acc[at, :] + found[i * 8 : (i + 1) * 8]

    stats[...] = jnp.zeros_like(stats)
    for n, piece in enumerate(split3(jnp.concatenate(lines, axis=0))):
        stats[pl.ds(n, 16, stride=16), :] = piece
        stats[pl.ds(8 + n, 16, stride=16), :] = pltpu.roll(piece, 64, 1)
    member = jnp.where(reqcol[...] == iota((128, 128), 1), 1.0, 0.0)
    sums = dot(sums, member, HIGH)
    spare[...] = jnp.concatenate([sums, jnp.zeros((96, 128), F32)], axis=0).T
    line = spare[pl.ds(0, 32, stride=2), :] + pltpu.roll(spare[pl.ds(1, 32, stride=2), :], 32, 1)
    for n, piece in enumerate(split3(line)):
        stats[pl.ds(3 + n, 32, stride=8), :] = piece
    packed[:, 64:72, :] = stats[...].astype(BF16).reshape(NREP, 8, 128)
    copies = []
    for n in range(4):
        rows = slice(n * 128, (n + 1) * 128)
        groups = [
            sum(accs[k * KVH + g][rows, :] for k in range(SPLIT)).reshape(16, 8, HD)
            for g in range(KVH)
        ]
        part = jnp.concatenate(groups, axis=1).reshape(8, 64, HD)
        packed[n * 8 : (n + 1) * 8, 0:64, :] = part.astype(BF16)
        copies.append(
            begin(packed.at[n * 8 : (n + 1) * 8], out.at[n * 8 : (n + 1) * 8], sem.at[n])
        )
    for copy in copies:
        copy.wait()


def combine_body(sel, recv, own, new_kv, out, acc, stats, factors):
    stats[...] = recv[:, 64:72, :].astype(F32).reshape(NREP * 8, 128)

    def stat(k):
        read = [stats[pl.ds(3 * k + n, 32, stride=8), :] for n in range(3)]
        return read[0] + read[1] + read[2]

    tops, sums = stat(0), stat(1)
    tops = jnp.concatenate([tops, pltpu.roll(tops, 96, 1)], axis=0)
    sums = jnp.concatenate([sums, pltpu.roll(sums, 96, 1)], axis=0)
    lane = iota((REQ, 128), 1)
    row = iota((REQ, 128), 0)
    head = lane < QH
    own_score = jnp.where(head, own[...], 0.0)
    best = own_score
    picks = [sel[0, 2 * p + s] for s in range(2) for p in range(NREP)]
    for c in range(64):
        best = jnp.where(row == picks[c], jnp.maximum(best, tops[c : c + 1]), best)
    factors[0:32, :] = best
    high = jnp.concatenate([factors[pl.ds(picks[c], 1), :] for c in range(64)], axis=0)
    scaled = jnp.where(iota((64, 128), 1) < QH, jnp.exp(tops - high), 0.0)
    sums = jnp.where(iota((64, 128), 1) < QH, sums, 0.0)
    added = scaled * sums
    total = jnp.exp(own_score - best)
    for c in range(64):
        total = total + jnp.where(row == picks[c], added[c : c + 1], 0.0)
    inverse = 1.0 / total
    own_factor = jnp.where(head, jnp.exp(own_score - best) * inverse, 0.0)
    factors[32:64, :] = inverse
    lines = [
        scaled
        * jnp.concatenate([factors[pl.ds(picks[c] + 32, 1), :] for c in range(64)], axis=0)
    ]
    turned = jnp.concatenate(lines + [own_factor, jnp.zeros((32, 128), F32)], axis=0).T
    turned = turned[:QH, :]
    for i in range(REQ):
        values = jnp.concatenate(
            [
                jnp.broadcast_to(
                    new_kv[i : i + 1, (KVH + g) * HD : (KVH + g + 1) * HD].astype(F32), (8, HD)
                )
                for g in range(KVH)
            ],
            axis=0,
        )
        acc[i * QH : (i + 1) * QH, :] = turned[:, 64 + i : 65 + i] * values
    for c in range(64):
        s, p = c // 32, c % 32
        at = pl.ds(pl.multiple_of(picks[c] * QH, QH), QH)
        given = recv[p, s * QH : (s + 1) * QH, :].astype(F32)
        acc[at, :] = acc[at, :] + turned[:, c : c + 1] * given
    for h in range(QH):
        out[:, h * HD : (h + 1) * HD] = acc[pl.ds(h, REQ, stride=QH), :].astype(BF16)


def exchange(values, axis):
    return lax.all_to_all(values, axis, split_axis=0, concat_axis=0, tiled=True)


def shards(
    hidden,
    base_query_rows,
    new_kv,
    adapter_down_matrix,
    adapter_up_matrix,
    holder,
    adapter_slot,
    kv_pages,
    mig_pages,
    page_owner,
    page_used,
):
    owner = in_hbm(page_owner.reshape(1, POOL))
    outgoing, pos = call(
        dispatch_body,
        [pltpu.HBM((256, WIDE), BF16), shape((1, 128), I32)],
        scratch=[
            pltpu.VMEM((REQ, 4 * QUART), BF16),
            pltpu.VMEM((1, REQ), I32),
            pltpu.VMEM((1, REQ), I32),
            pltpu.VMEM((1, POOL), I32),
            pltpu.VMEM((256, WIDE), BF16),
            sems(8),
        ],
        ins=[ANY] * 4,
        out_specs=[ANY, VM],
        moved=2 << 20,
    )(in_hbm(hidden), in_hbm(holder.reshape(1, REQ)), in_hbm(adapter_slot.reshape(1, REQ)), owner)
    rows_in = exchange(outgoing.reshape(NREP, 8, WIDE), "replica")

    down = in_hbm(adapter_down_matrix)
    flat_pages = in_hbm(kv_pages.reshape(96 * PAGE, 1024))
    *leaving, early = call(
        leave_body,
        [pltpu.VMEM((64, 1024), BF16)] * NBUC
        + [pltpu.VMEM((DHALF, 256), BF16)],
        scratch=[sems(33)],
        ins=[SM] + [ANY] * 3,
        moved=6 << 20,
    )(
        mig_pages.reshape(1, 32),
        flat_pages,
        down,
        pos,
    )
    arrived = [leaving[0]] + [
        lax.ppermute(leaving[k], "bucket", [(s, s ^ k) for s in range(NBUC)]) for k in range(1, NBUC)
    ]
    arrived = [in_hbm(one) for one in arrived]

    raised, sel = call(
        adapter_body,
        [pltpu.HBM((2048, 128), BF16), shape((1, 128), I32)],
        scratch=[
            pltpu.VMEM((2048, 128), F32),
            pltpu.VMEM((2048, 128), BF16),
            pltpu.VMEM((DHALF, 256), BF16),
            pltpu.VMEM(adapter_up_matrix.shape, BF16),
            pltpu.VMEM((2 * QUART, 128), F32),
            sems(9),
        ],
        ins=[VM, VM] + [ANY] * (2 + NBUC),
        out_specs=[ANY, VM],
        flops=1 << 30,
        moved=8 << 20,
    )(
        in_vmem(rows_in.reshape(256, WIDE)),
        in_vmem(early),
        down,
        in_hbm(adapter_up_matrix),
        *arrived,
    )
    returned = exchange(raised.reshape(NREP, 64, 128), "replica")
    rowid, spread, reqcol, based, keys, values = call(
        prepare_body,
        [
            shape((1, 128), I32),
            pltpu.VMEM((8, POOL * PAGE), I32),
            pltpu.VMEM((128, 128), I32),
            pltpu.VMEM((REQ * QH, HD), BF16),
            pltpu.VMEM((BLOCKS * KVH * HD, 128), BF16),
            pltpu.HBM((POOL * PAGE, KVH * HD), BF16),
        ],
        scratch=[
            pltpu.VMEM((1, POOL), I32),
            pltpu.VMEM((1, POOL), I32),
            pltpu.VMEM((96 * PAGE, 1024), BF16),
            pltpu.VMEM((32 * PAGE, 1024), BF16),
            pltpu.VMEM((REQ, QH * HD), BF16),
            pltpu.VMEM((REQ * QH, HD), F32),
            pltpu.VMEM((POOL * PAGE, KVH * HD), BF16),
            sems(13),
        ],
        ins=[ANY] * (5 + NBUC),
        out_specs=[VM] * 5 + [ANY],
        moved=8 << 20,
    )(
        owner,
        in_hbm(page_used.reshape(1, POOL)),
        flat_pages,
        in_hbm(base_query_rows),
        sel,
        *arrived,
    )

    queries, asked = call(
        query_body,
        [pltpu.VMEM((REQ * QH, HD), BF16), pltpu.HBM((2048, 128), BF16)],
        scratch=[pltpu.VMEM((2048, 128), BF16), sems(4)],
        ins=[SM, SM, VM, VM],
        out_specs=[VM, ANY],
    )(pos, sel, in_vmem(returned.reshape(2048, 128)), in_vmem(based))
    recv = exchange(asked.reshape(NREP, 64, 128), "replica")
    (own,) = call(
        own_body,
        [pltpu.VMEM((REQ, 128), F32)],
        scratch=[pltpu.VMEM(new_kv.shape, BF16), sems(1)],
        ins=[VM, ANY],
    )(in_vmem(queries), in_hbm(new_kv))

    (partial,) = call(
        attend_body,
        [pltpu.HBM((NREP, CROWS, 128), BF16)],
        scratch=[
            pltpu.VMEM((2048, 128), F32),
            pltpu.VMEM((QH, POOL * PAGE), F32),
            pltpu.VMEM((128, 128), F32),
            pltpu.VMEM((256, 128), F32),
            pltpu.VMEM((NREP, CROWS, 128), BF16),
            pltpu.VMEM((POOL * PAGE, KVH * HD), BF16),
            sems(5),
        ]
        + [pltpu.VMEM((512, 128), F32)] * (SPLIT * KVH),
        ins=[SM] + [VM] * 4 + [ANY] * 2,
        out_specs=[ANY],
        flops=1 << 29,
        moved=6 << 20,
    )(
        rowid,
        in_vmem(spread),
        in_vmem(reqcol),
        in_vmem(recv.reshape(2048, 128)),
        in_vmem(keys),
        own,
        in_hbm(values),
    )
    parts = exchange(partial, "replica")
    (fresh,) = call(
        fresh_body,
        [pltpu.VMEM(new_kv.shape, BF16)],
        scratch=[sems(1)],
        ins=[ANY] * 2,
    )(in_hbm(new_kv), in_hbm(partial))

    return call(
        combine_body,
        [shape((REQ, QH * HD), BF16)],
        scratch=[
            pltpu.VMEM((REQ * QH, HD), F32),
            pltpu.VMEM((256, 128), F32),
            pltpu.VMEM((64, 128), F32),
        ],
        ins=[SM, VM, VM, VM],
    )(sel, in_vmem(parts), in_vmem(own), in_vmem(fresh))[0]


def solution(mesh):
    rows = P(("bucket", "replica"), None)
    flat = P(("bucket", "replica"))
    placed = (
        rows,
        rows,
        rows,
        P(None, ("bucket", "replica")),
        rows,
        rows,
        flat,
        P(("bucket", "replica"), None, None),
        flat,
        flat,
        flat,
    )
    return jax.shard_map(
        shards, mesh=mesh, in_specs=placed, out_specs=rows, check_vma=False
    )
```

```python
import jax
import jax.numpy as jnp
from jax import lax
from jax.experimental import pallas as pl
from jax.experimental.pallas import tpu as pltpu
from jax.sharding import PartitionSpec as P

QH = 32
KVH = 4
HD = 128
RANK = 64
PAGE = 16
REQ = 32
NREP = 32
NBUC = 8
POOL = 128
QUART = 2048
WIDE = QUART + 128
BLOCKS = 16
CROWS = 72
DHALF = 4096
SPLIT = 1
SCALE = HD ** -0.5
LOW = -3e38
NEG = -1e30
HIGH = lax.Precision.HIGHEST
F32 = jnp.float32
BF16 = jnp.bfloat16
I32 = jnp.int32
VM = pl.BlockSpec(memory_space=pltpu.VMEM)
ANY = pl.BlockSpec(memory_space=pl.ANY)
SM = pl.BlockSpec(memory_space=pltpu.SMEM)


def iota(shape, axis):
    return lax.broadcasted_iota(I32, shape, axis)


def dot(left, right, precision=None):
    return jnp.dot(left, right, preferred_element_type=F32, precision=precision)


def call(body, outs, scratch=(), ins=None, out_specs=None, mib=24, flops=1 << 20, moved=1 << 20):
    return pl.pallas_call(
        body,
        out_shape=tuple(outs),
        in_specs=ins,
        out_specs=tuple(out_specs or [VM] * len(outs)),
        scratch_shapes=list(scratch),
        compiler_params=pltpu.CompilerParams(vmem_limit_bytes=mib << 20),
        cost_estimate=pl.CostEstimate(flops=flops, bytes_accessed=moved, transcendentals=0),
    )


def in_hbm(values):
    return pltpu.with_memory_space_constraint(values, pltpu.HBM)


def in_vmem(values):
    return pltpu.with_memory_space_constraint(values, pltpu.VMEM)


def begin(source, target, sem):
    copy = pltpu.make_async_copy(source, target, sem)
    copy.start()
    return copy


def sems(count):
    return pltpu.SemaphoreType.DMA((count,))


def shape(dims, kind):
    return jax.ShapeDtypeStruct(dims, kind)


def dispatch_body(hidden_in, holder_in, slot_in, owner_in, out, pos, hidden, holder, slot, owner, made, sem):
    small = [
        begin(source, target, sem.at[n])
        for n, (source, target) in enumerate(
            ((holder_in, holder), (slot_in, slot), (owner_in, owner))
        )
    ]
    large = begin(hidden_in, hidden, sem.at[3])
    for copy in small:
        copy.wait()
    square = (REQ, REQ)
    col = jnp.sum(
        jnp.where(iota(square, 0) == iota(square, 1), holder[...], 0), axis=1, keepdims=True
    )
    col4 = jnp.concatenate([col] * 4, axis=0)
    square = (128, 128)
    target = jnp.sum(jnp.where(iota(square, 0) == iota(square, 1), col4, 0), axis=0, keepdims=True)
    earlier = (col == target) & (iota((REQ, 128), 0) < (iota((REQ, 128), 1) & 31))
    rank = jnp.sum(jnp.where(earlier, 1, 0), axis=0, keepdims=True)
    place = 2 * target + rank
    pos[...] = place
    full = (256, 128)
    row, lane = iota(full, 0), iota(full, 1)
    at_place = (row >> 2) == place
    onehot = jnp.where(at_place & ((row & 3) == (lane >> 5)), 1.0, 0.0).astype(BF16)
    slot_col = jnp.sum(jnp.where(at_place[:, :REQ], slot[...], 0), axis=1, keepdims=True)
    own = owner[...]
    here = (own >> 5) == (row >> 3)
    local = own & 31
    least = jnp.min(jnp.where(here, local, 99), axis=1, keepdims=True)
    most = jnp.max(jnp.where(here, local, -1), axis=1, keepdims=True)
    second = ((row >> 2) & 1) == 1
    chosen = jnp.where(second, most, least)
    meta = jnp.where(lane == 0, slot_col, jnp.where(lane == 1, chosen, 0))
    made[:, QUART:] = meta.astype(F32).astype(BF16)
    large.wait()
    stacked = jnp.concatenate([hidden[:, q * QUART : (q + 1) * QUART] for q in range(4)], axis=0)
    copies = []
    for n in range(4):
        rows = slice(n * 64, (n + 1) * 64)
        made[rows, :QUART] = dot(onehot[rows], stacked).astype(BF16)
        copies.append(begin(made.at[n * 64 : (n + 1) * 64], out.at[n * 64 : (n + 1) * 64], sem.at[4 + n]))
    for copy in copies:
        copy.wait()


def prepare_body(owner_in, used_in, pages_in, after, *rest):
    given, outs, scratch = rest[:NBUC], rest[NBUC : NBUC + 5], rest[NBUC + 5 :]
    rowid, spread, reqcol, keys, values_out = outs
    owner, used, pages, pieces, values, sem = scratch
    copies = [
        begin(source, target, sem.at[n])
        for n, (source, target) in enumerate(
            ((owner_in, owner), (used_in, used), (pages_in, pages))
        )
    ]
    arrived = [pieces.at[k * 64 : (k + 1) * 64] for k in range(NBUC)]
    copies += [begin(given[k], arrived[k], sem.at[4 + k]) for k in range(NBUC)]
    copies[0].wait()
    copies[1].wait()
    own = owner[...]
    square = (128, 128)
    row, lane = iota(square, 0), iota(square, 1)
    own_col = jnp.sum(jnp.where(row == lane, own, 0), axis=1, keepdims=True)
    least = jnp.min(jnp.where((own_col >> 5) == (own >> 5), own_col, 1 << 20), axis=0, keepdims=True)
    ids = 2 * (own >> 5) + jnp.where(own > least, 1, 0)
    both = jnp.where(
        iota((16, 128), 0) == 0, ids, jnp.where(iota((16, 128), 0) == 1, used[...], 0)
    ).astype(F32).astype(BF16)
    turn = lax.axis_index("bucket") << 2

    def moved(slot):
        return jnp.where(slot < 96, slot, slot ^ turn)

    one = jnp.where(row == moved(lane), 1.0, 0.0).astype(BF16)
    rowid[...] = dot(both, one)[:1].astype(I32)
    wide = (128, POOL * PAGE)
    onehot = jnp.where(iota(wide, 0) == moved(iota(wide, 1) >> 4), 1.0, 0.0).astype(BF16)
    spread[...] = dot(both, onehot)[:8].astype(I32)
    slot = ((row & 15) << 3) + (row >> 4)
    reqcol[...] = jnp.broadcast_to(
        jnp.sum(jnp.where(lane == moved(slot), ids, 0), axis=1, keepdims=True), square
    )
    for copy in copies[2:]:
        copy.wait()
    for b in range(12):
        rows = slice(b * 128, (b + 1) * 128)
        values[rows, :] = pages[rows, KVH * HD :]
    for k in range(NBUC):
        values[(24 + k) * 64 : (25 + k) * 64, :] = arrived[k][:, KVH * HD :]
    store = begin(values, values_out, sem.at[12])
    for b in range(BLOCKS):
        for g in range(KVH):
            cut = slice(g * HD, (g + 1) * HD)
            if b < 12:
                block = pages[b * 128 : (b + 1) * 128, cut]
            else:
                block = jnp.concatenate([one[:, cut] for one in arrived[2 * b - 24 : 2 * b - 22]], axis=0)
            keys[(b * KVH + g) * HD : (b * KVH + g + 1) * HD, :] = block.T
    store.wait()


def leave_body(mig, pages, down_in, base_in, after, *rest):
    outs, (down, based, base, turned, sem) = rest[:NBUC], rest[NBUC:]
    load = begin(base_in, base, sem.at[33])
    me = lax.axis_index("bucket")
    copies = []
    for k in range(NBUC):
        for j in range(4):
            page = mig[0, (me ^ k) * 4 + j]
            copies.append(
                begin(
                    pages.at[pl.ds(pl.multiple_of(page * PAGE, PAGE), PAGE)],
                    outs[k].at[pl.ds(j * PAGE, PAGE)],
                    sem.at[k * 4 + j],
                )
            )
    copies.append(begin(down_in.at[:DHALF], down, sem.at[32]))
    load.wait()
    for h in range(QH):
        turned[pl.ds(h, REQ, stride=QH), :] = base[:, h * HD : (h + 1) * HD].astype(F32)
    based[...] = turned[...].astype(BF16)
    for copy in copies:
        copy.wait()


def adapter_body(rows, early, down_in, up_in, *rest):
    raised, sel, spare, down, up, apart, sem = rest[NBUC:]
    loads = [
        begin(down_in.at[DHALF + n * 1024 : DHALF + (n + 1) * 1024], down.at[n * 1024 : (n + 1) * 1024], sem.at[4 + n])
        for n in range(4)
    ]
    load_up = begin(up_in, up, sem.at[8])
    lowered = jnp.zeros((64, 256), F32)
    for n in range(QUART // 128):
        apart[n * 256 : (n + 1) * 256, :] = rows[:, n * 128 : (n + 1) * 128].astype(F32)
    for q in range(4):
        data = jnp.concatenate(
            [apart[pl.ds(n * 256 + q, 64, stride=4), :] for n in range(QUART // 128)], axis=1
        ).astype(BF16)
        if q < 2:
            weights = early[q * QUART : (q + 1) * QUART, :]
        else:
            loads[2 * q - 4].wait()
            loads[2 * q - 3].wait()
            weights = down[(q - 2) * QUART : (q - 1) * QUART, :]
        lowered = lowered + dot(data, weights)
    first = jnp.where(iota((64, 256), 1) == 4 * iota((64, 256), 0), 1.0, 0.0).astype(BF16)
    meta = dot(first, rows[:, QUART:]).astype(I32)
    sel[...] = jnp.sum(
        jnp.where(iota((64, 128), 0) == iota((64, 128), 1), meta[:, 1:2], 0), axis=0, keepdims=True
    )
    chosen = meta[:, 0:1] == (iota((64, 256), 1) >> 6)
    kept = jnp.where(chosen, lowered, 0.0).astype(BF16)
    load_up.wait()
    for n in range(16):
        piece = dot(kept, up[:, n * 256 : (n + 1) * 256])
        spare[pl.ds(2 * n, 64, stride=32), :] = piece[:, :128]
        spare[pl.ds(2 * n + 1, 64, stride=32), :] = piece[:, 128:]
    raised[...] = spare[...].astype(BF16)


def query_body(pos, sel, delta, based, queries, out, packed, sem):
    for i in range(REQ):
        from_row = pl.multiple_of(pos[0, i] * QH, QH)
        rows = slice(i * QH, (i + 1) * QH)
        queries[rows, :] = (based[rows, :].astype(F32) + delta[pl.ds(from_row, QH), :].astype(F32)).astype(BF16)
    copies = []
    for c in range(2 * NREP):
        from_row = pl.multiple_of(sel[0, c] * QH, QH)
        packed[c * QH : (c + 1) * QH, :] = queries[pl.ds(from_row, QH), :]
        if c % 16 == 15:
            n = c // 16
            copies.append(
                begin(packed.at[n * 512 : (n + 1) * 512], out.at[n * 512 : (n + 1) * 512], sem.at[n])
            )
    for copy in copies:
        copy.wait()


def own_body(queries, new_in, own, new_kv, sem):
    begin(new_in, new_kv, sem.at[0]).wait()
    lane = iota((QH, 128), 1)
    columns = jnp.zeros((QH, 128), F32)
    for i in range(REQ):
        query = queries[i * QH : (i + 1) * QH, :].astype(F32)
        keys = jnp.concatenate(
            [
                jnp.broadcast_to(new_kv[i : i + 1, g * HD : (g + 1) * HD].astype(F32), (8, HD))
                for g in range(KVH)
            ],
            axis=0,
        )
        columns = jnp.where(lane == i, jnp.sum(query * keys, axis=1, keepdims=True), columns)
    padded = jnp.concatenate([columns, jnp.zeros((96, 128), F32)], axis=0)
    own[...] = padded.T[:REQ, :] * SCALE


def merge_pages(blocks):
    lane = iota((QH, 128), 1)
    for step in (8, 4, 2, 1):
        upper = (lane & step) != 0
        merged = []
        for first, second in zip(blocks[:step], blocks[step:]):
            stay = jnp.where(upper, second, first)
            swap = jnp.where(upper, first, second)
            swap = jnp.where(upper, pltpu.roll(swap, step, 1), pltpu.roll(swap, 128 - step, 1))
            merged.append(jnp.maximum(stay, swap))
        blocks = merged
    return blocks[0]


def split3(values):
    high = values.astype(BF16).astype(F32)
    rest = values - high
    middle = rest.astype(BF16).astype(F32)
    return high, middle, rest - middle


def attend_body(
    rowid, spread, reqcol, recv, keys, values_in, packed,
    qf, cs, spare, stats, values, sem, *accs,
):
    load_values = begin(values_in, values, sem.at[0])
    qf[...] = recv[...].astype(F32)
    for acc in accs:
        acc[...] = jnp.zeros_like(acc)
    page8 = iota((8, 128), 1) >> 4
    ids = [rowid[0, p] * QH for p in range(POOL)]
    for b in range(BLOCKS):
        cut = slice(b * 128, (b + 1) * 128)
        for g in range(KVH):
            query = jnp.concatenate(
                [qf[pl.ds(pl.multiple_of(ids[b * 8 + i] + g * 8, 8), 8), :] for i in range(8)], axis=0
            ).astype(BF16)
            found = dot(query, keys[(b * KVH + g) * HD : (b * KVH + g + 1) * HD, :])
            kept = found[0:8]
            for i in range(1, 8):
                kept = jnp.where(page8 == i, found[i * 8 : (i + 1) * 8], kept)
            cs[g * 8 : (g + 1) * 8, cut] = kept

    spot = iota((QH, 128), 1) & 15
    valid, blocks = [], []
    for b in range(BLOCKS):
        cut = slice(b * 128, (b + 1) * 128)
        valid.append(spot < spread[1:2, cut])
        blocks.append(jnp.where(valid[b], cs[:, cut] * SCALE, NEG))
        cs[:, cut] = blocks[b]
    merged = merge_pages(blocks)
    turned = jnp.concatenate([merged] * 4, axis=0).T
    which = reqcol[...] - (iota((128, 128), 1) >> 5)
    tops = jnp.full((128, 128), LOW, F32)
    lines = []
    for n in range(16):
        mine = which == 4 * n
        top = jnp.max(jnp.where(mine, turned, LOW), axis=0, keepdims=True)
        lines.append(top)
        tops = jnp.where(mine, top, tops)
    tops = jnp.maximum(tops, pltpu.roll(tops, 32, 1))
    tops = jnp.maximum(tops, pltpu.roll(tops, 64, 1)).T[:QH, :]
    pieces = jnp.concatenate(split3(tops), axis=0).astype(BF16)
    place = iota((128, 128), 0) - ((iota((128, 128), 1) >> 4) << 4)
    placed = iota((128, 128), 1) - ((iota((128, 128), 0) >> 4) << 4)
    sums = jnp.zeros((QH, 128), F32)
    for b in range(BLOCKS):
        cut = slice(b * 128, (b + 1) * 128)
        spread_tops = dot(pieces, jnp.where(place == b, 1.0, 0.0).astype(BF16))
        top = spread_tops[0:32] + spread_tops[32:64] + spread_tops[64:96]
        weight = jnp.where(valid[b], jnp.exp(cs[:, cut] - top), 0.0).astype(BF16)
        cs[:, cut] = weight.astype(F32)
        sums = sums + dot(weight, jnp.where(placed == b, 1.0, 0.0).astype(BF16))

    load_values.wait()
    for b in range(BLOCKS):
        cut = slice(b * 128, (b + 1) * 128)
        for g in range(KVH):
            weight = cs[g * 8 : (g + 1) * 8, cut]
            spread_weight = jnp.concatenate(
                [jnp.where(page8 == i, weight, 0.0) for i in range(8)], axis=0
            ).astype(BF16)
            found = dot(spread_weight, values[cut, g * HD : (g + 1) * HD])
            for i in range(8):
                at = pl.ds(pl.multiple_of(ids[b * 8 + i] // 4, 8), 8)
                acc = accs[(i % SPLIT) * KVH + g]
                acc[at, :] = acc[at, :] + found[i * 8 : (i + 1) * 8]

    stats[...] = jnp.zeros_like(stats)
    for n, piece in enumerate(split3(jnp.concatenate(lines, axis=0))):
        stats[pl.ds(n, 16, stride=16), :] = piece
        stats[pl.ds(8 + n, 16, stride=16), :] = pltpu.roll(piece, 64, 1)
    member = jnp.where(reqcol[...] == iota((128, 128), 1), 1.0, 0.0)
    sums = dot(sums, member, HIGH)
    spare[...] = jnp.concatenate([sums, jnp.zeros((96, 128), F32)], axis=0).T
    line = spare[pl.ds(0, 32, stride=2), :] + pltpu.roll(spare[pl.ds(1, 32, stride=2), :], 32, 1)
    for n, piece in enumerate(split3(line)):
        stats[pl.ds(3 + n, 32, stride=8), :] = piece
    packed[:, 64:72, :] = stats[...].astype(BF16).reshape(NREP, 8, 128)
    for n in range(4):
        rows = slice(n * 128, (n + 1) * 128)
        groups = [
            sum(accs[k * KVH + g][rows, :] for k in range(SPLIT)).reshape(16, 8, HD)
            for g in range(KVH)
        ]
        part = jnp.concatenate(groups, axis=1).reshape(8, 64, HD)
        packed[n * 8 : (n + 1) * 8, 0:64, :] = part.astype(BF16)


def combine_body(sel, recv, own, new_kv, out, acc, stats, factors):
    stats[...] = recv[:, 64:72, :].astype(F32).reshape(NREP * 8, 128)

    def stat(k):
        read = [stats[pl.ds(3 * k + n, 32, stride=8), :] for n in range(3)]
        return read[0] + read[1] + read[2]

    tops, sums = stat(0), stat(1)
    tops = jnp.concatenate([tops, pltpu.roll(tops, 96, 1)], axis=0)
    sums = jnp.concatenate([sums, pltpu.roll(sums, 96, 1)], axis=0)
    lane = iota((REQ, 128), 1)
    row = iota((REQ, 128), 0)
    head = lane < QH
    own_score = jnp.where(head, own[...], 0.0)
    best = own_score
    picks = [sel[0, 2 * p + s] for s in range(2) for p in range(NREP)]
    for c in range(64):
        best = jnp.where(row == picks[c], jnp.maximum(best, tops[c : c + 1]), best)
    factors[0:32, :] = best
    high = jnp.concatenate([factors[pl.ds(picks[c], 1), :] for c in range(64)], axis=0)
    scaled = jnp.where(iota((64, 128), 1) < QH, jnp.exp(tops - high), 0.0)
    sums = jnp.where(iota((64, 128), 1) < QH, sums, 0.0)
    added = scaled * sums
    total = jnp.exp(own_score - best)
    for c in range(64):
        total = total + jnp.where(row == picks[c], added[c : c + 1], 0.0)
    inverse = 1.0 / total
    own_factor = jnp.where(head, jnp.exp(own_score - best) * inverse, 0.0)
    factors[32:64, :] = inverse
    lines = [
        scaled
        * jnp.concatenate([factors[pl.ds(picks[c] + 32, 1), :] for c in range(64)], axis=0)
    ]
    turned = jnp.concatenate(lines + [own_factor, jnp.zeros((32, 128), F32)], axis=0).T
    turned = turned[:QH, :]
    for i in range(REQ):
        values = jnp.concatenate(
            [
                jnp.broadcast_to(
                    new_kv[i : i + 1, (KVH + g) * HD : (KVH + g + 1) * HD].astype(F32), (8, HD)
                )
                for g in range(KVH)
            ],
            axis=0,
        )
        acc[i * QH : (i + 1) * QH, :] = turned[:, 64 + i : 65 + i] * values
    for c in range(64):
        s, p = c // 32, c % 32
        at = pl.ds(pl.multiple_of(picks[c] * QH, QH), QH)
        given = recv[p, s * QH : (s + 1) * QH, :].astype(F32)
        acc[at, :] = acc[at, :] + turned[:, c : c + 1] * given
    for h in range(QH):
        out[:, h * HD : (h + 1) * HD] = acc[pl.ds(h, REQ, stride=QH), :].astype(BF16)


def exchange(values, axis):
    return lax.all_to_all(values, axis, split_axis=0, concat_axis=0, tiled=True)


def shards(
    hidden,
    base_query_rows,
    new_kv,
    adapter_down_matrix,
    adapter_up_matrix,
    holder,
    adapter_slot,
    kv_pages,
    mig_pages,
    page_owner,
    page_used,
):
    owner = in_hbm(page_owner.reshape(1, POOL))
    outgoing, pos = call(
        dispatch_body,
        [pltpu.HBM((256, WIDE), BF16), shape((1, 128), I32)],
        scratch=[
            pltpu.VMEM((REQ, 4 * QUART), BF16),
            pltpu.VMEM((1, REQ), I32),
            pltpu.VMEM((1, REQ), I32),
            pltpu.VMEM((1, POOL), I32),
            pltpu.VMEM((256, WIDE), BF16),
            sems(8),
        ],
        ins=[ANY] * 4,
        out_specs=[ANY, VM],
        moved=2 << 20,
    )(in_hbm(hidden), in_hbm(holder.reshape(1, REQ)), in_hbm(adapter_slot.reshape(1, REQ)), owner)
    rows_in = exchange(outgoing.reshape(NREP, 8, WIDE), "replica")

    down = in_hbm(adapter_down_matrix)
    flat_pages = in_hbm(kv_pages.reshape(96 * PAGE, 1024))
    *leaving, early, based = call(
        leave_body,
        [pltpu.VMEM((64, 1024), BF16)] * NBUC
        + [pltpu.VMEM((DHALF, 256), BF16), pltpu.VMEM((REQ * QH, HD), BF16)],
        scratch=[pltpu.VMEM((REQ, QH * HD), BF16), pltpu.VMEM((REQ * QH, HD), F32), sems(34)],
        ins=[SM] + [ANY] * 4,
        moved=6 << 20,
    )(
        mig_pages.reshape(1, 32),
        flat_pages,
        down,
        in_hbm(base_query_rows),
        pos,
    )
    arrived = [leaving[0]] + [
        lax.ppermute(leaving[k], "bucket", [(s, s ^ k) for s in range(NBUC)]) for k in range(1, NBUC)
    ]
    arrived = [in_hbm(one) for one in arrived]

    raised, sel = call(
        adapter_body,
        [pltpu.VMEM((2048, 128), BF16), shape((1, 128), I32)],
        scratch=[
            pltpu.VMEM((2048, 128), F32),
            pltpu.VMEM((DHALF, 256), BF16),
            pltpu.VMEM(adapter_up_matrix.shape, BF16),
            pltpu.VMEM((2 * QUART, 128), F32),
            sems(9),
        ],
        ins=[VM, VM] + [ANY] * (2 + NBUC),
        flops=1 << 30,
        moved=8 << 20,
    )(
        in_vmem(rows_in.reshape(256, WIDE)),
        in_vmem(early),
        down,
        in_hbm(adapter_up_matrix),
        *arrived,
    )
    returned = exchange(raised.reshape(NREP, 64, 128), "replica")
    queries, asked = call(
        query_body,
        [pltpu.VMEM((REQ * QH, HD), BF16), pltpu.HBM((2048, 128), BF16)],
        scratch=[pltpu.VMEM((2048, 128), BF16), sems(4)],
        ins=[SM, SM, VM, VM],
        out_specs=[VM, ANY],
    )(pos, sel, in_vmem(returned.reshape(2048, 128)), in_vmem(based))
    recv = exchange(asked.reshape(NREP, 64, 128), "replica")
    own, fresh = call(
        own_body,
        [pltpu.VMEM((REQ, 128), F32), pltpu.VMEM(new_kv.shape, BF16)],
        scratch=[sems(1)],
        ins=[VM, ANY],
    )(in_vmem(queries), in_hbm(new_kv))
    rowid, spread, reqcol, keys, values = call(
        prepare_body,
        [
            shape((1, 128), I32),
            pltpu.VMEM((8, POOL * PAGE), I32),
            pltpu.VMEM((128, 128), I32),
            pltpu.VMEM((BLOCKS * KVH * HD, 128), BF16),
            pltpu.HBM((POOL * PAGE, KVH * HD), BF16),
        ],
        scratch=[
            pltpu.VMEM((1, POOL), I32),
            pltpu.VMEM((1, POOL), I32),
            pltpu.VMEM((96 * PAGE, 1024), BF16),
            pltpu.VMEM((32 * PAGE, 1024), BF16),
            pltpu.VMEM((POOL * PAGE, KVH * HD), BF16),
            sems(13),
        ],
        ins=[ANY] * (4 + NBUC),
        out_specs=[VM] * 4 + [ANY],
        moved=8 << 20,
    )(
        owner,
        in_hbm(page_used.reshape(1, POOL)),
        flat_pages,
        own,
        *arrived,
    )

    (partial,) = call(
        attend_body,
        [pltpu.VMEM((NREP, CROWS, 128), BF16)],
        scratch=[
            pltpu.VMEM((2048, 128), F32),
            pltpu.VMEM((QH, POOL * PAGE), F32),
            pltpu.VMEM((128, 128), F32),
            pltpu.VMEM((256, 128), F32),
            pltpu.VMEM((POOL * PAGE, KVH * HD), BF16),
            sems(1),
        ]
        + [pltpu.VMEM((512, 128), F32)] * (SPLIT * KVH),
        ins=[SM] + [VM] * 4 + [ANY],
        flops=1 << 29,
        moved=6 << 20,
    )(
        rowid,
        in_vmem(spread),
        in_vmem(reqcol),
        in_vmem(recv.reshape(2048, 128)),
        in_vmem(keys),
        in_hbm(values),
    )
    parts = exchange(partial, "replica")

    return call(
        combine_body,
        [shape((REQ, QH * HD), BF16)],
        scratch=[
            pltpu.VMEM((REQ * QH, HD), F32),
            pltpu.VMEM((256, 128), F32),
            pltpu.VMEM((64, 128), F32),
        ],
        ins=[SM, VM, VM, VM],
    )(sel, in_vmem(parts), in_vmem(own), in_vmem(fresh))[0]


def solution(mesh):
    rows = P(("bucket", "replica"), None)
    flat = P(("bucket", "replica"))
    placed = (
        rows,
        rows,
        rows,
        P(None, ("bucket", "replica")),
        rows,
        rows,
        flat,
        P(("bucket", "replica"), None, None),
        flat,
        flat,
        flat,
    )
    return jax.shard_map(
        shards, mesh=mesh, in_specs=placed, out_specs=rows, check_vma=False
    )
```

```python
import jax
import jax.numpy as jnp
from jax import lax
from jax.experimental import pallas as pl
from jax.experimental.pallas import tpu as pltpu
from jax.sharding import PartitionSpec as P

QH = 32
KVH = 4
HD = 128
RANK = 64
PAGE = 16
REQ = 32
NREP = 32
NBUC = 8
POOL = 128
QUART = 2048
WIDE = QUART + 128
BLOCKS = 16
CROWS = 72
DHALF = 4096
MOVED = 7
SOON = 7
SPLIT = 1
SCALE = HD ** -0.5
LOW = -3e38
NEG = -1e30
HIGH = lax.Precision.HIGHEST
F32 = jnp.float32
BF16 = jnp.bfloat16
I32 = jnp.int32
VM = pl.BlockSpec(memory_space=pltpu.VMEM)
ANY = pl.BlockSpec(memory_space=pl.ANY)
SM = pl.BlockSpec(memory_space=pltpu.SMEM)


def iota(shape, axis):
    return lax.broadcasted_iota(I32, shape, axis)


def dot(left, right, precision=None):
    return jnp.dot(left, right, preferred_element_type=F32, precision=precision)


def call(body, outs, scratch=(), ins=None, out_specs=None, mib=24, flops=1 << 20, moved=1 << 20):
    return pl.pallas_call(
        body,
        out_shape=tuple(outs),
        in_specs=ins,
        out_specs=tuple(out_specs or [VM] * len(outs)),
        scratch_shapes=list(scratch),
        compiler_params=pltpu.CompilerParams(vmem_limit_bytes=mib << 20),
        cost_estimate=pl.CostEstimate(flops=flops, bytes_accessed=moved, transcendentals=0),
    )


def in_hbm(values):
    return pltpu.with_memory_space_constraint(values, pltpu.HBM)


def in_vmem(values):
    return pltpu.with_memory_space_constraint(values, pltpu.VMEM)


def begin(source, target, sem):
    copy = pltpu.make_async_copy(source, target, sem)
    copy.start()
    return copy


def sems(count):
    return pltpu.SemaphoreType.DMA((count,))


def shape(dims, kind):
    return jax.ShapeDtypeStruct(dims, kind)


def dispatch_body(hidden_in, holder_in, slot_in, owner_in, out, pos, hidden, holder, slot, owner, made, sem):
    small = [
        begin(source, target, sem.at[n])
        for n, (source, target) in enumerate(
            ((holder_in, holder), (slot_in, slot), (owner_in, owner))
        )
    ]
    large = begin(hidden_in, hidden, sem.at[3])
    for copy in small:
        copy.wait()
    square = (REQ, REQ)
    col = jnp.sum(
        jnp.where(iota(square, 0) == iota(square, 1), holder[...], 0), axis=1, keepdims=True
    )
    col4 = jnp.concatenate([col] * 4, axis=0)
    square = (128, 128)
    target = jnp.sum(jnp.where(iota(square, 0) == iota(square, 1), col4, 0), axis=0, keepdims=True)
    earlier = (col == target) & (iota((REQ, 128), 0) < (iota((REQ, 128), 1) & 31))
    rank = jnp.sum(jnp.where(earlier, 1, 0), axis=0, keepdims=True)
    place = 2 * target + rank
    pos[...] = place
    full = (256, 128)
    row, lane = iota(full, 0), iota(full, 1)
    at_place = (row >> 2) == place
    onehot = jnp.where(at_place & ((row & 3) == (lane >> 5)), 1.0, 0.0).astype(BF16)
    slot_col = jnp.sum(jnp.where(at_place[:, :REQ], slot[...], 0), axis=1, keepdims=True)
    own = owner[...]
    here = (own >> 5) == (row >> 3)
    local = own & 31
    least = jnp.min(jnp.where(here, local, 99), axis=1, keepdims=True)
    most = jnp.max(jnp.where(here, local, -1), axis=1, keepdims=True)
    second = ((row >> 2) & 1) == 1
    chosen = jnp.where(second, most, least)
    meta = jnp.where(lane == 0, slot_col, jnp.where(lane == 1, chosen, 0))
    made[:, QUART:] = meta.astype(F32).astype(BF16)
    large.wait()
    stacked = jnp.concatenate([hidden[:, q * QUART : (q + 1) * QUART] for q in range(4)], axis=0)
    copies = []
    for n in range(4):
        rows = slice(n * 64, (n + 1) * 64)
        made[rows, :QUART] = dot(onehot[rows], stacked).astype(BF16)
        copies.append(begin(made.at[n * 64 : (n + 1) * 64], out.at[n * 64 : (n + 1) * 64], sem.at[4 + n]))
    for copy in copies:
        copy.wait()


def prepare_body(mig, owner_in, used_in, pages_in, after, *rest):
    given, outs, scratch = rest[:MOVED], rest[MOVED : MOVED + 5], rest[MOVED + 5 :]
    rowid, spread, reqcol, keys, values_out = outs
    owner, used, pages, pieces, values, sem = scratch
    copies = [
        begin(source, target, sem.at[n])
        for n, (source, target) in enumerate(
            ((owner_in, owner), (used_in, used), (pages_in, pages))
        )
    ]
    arrived = [pieces.at[k * 64 : (k + 1) * 64] for k in range(NBUC)]
    copies += [begin(given[k - 1], arrived[k], sem.at[4 + k]) for k in range(1, NBUC)]
    for j in range(4):
        page = mig[0, lax.axis_index("bucket") * 4 + j]
        rows = pl.ds(pl.multiple_of(page * PAGE, PAGE), PAGE)
        copies.append(begin(pages_in.at[rows], pieces.at[pl.ds(j * PAGE, PAGE)], sem.at[13 + j]))
    copies[0].wait()
    copies[1].wait()
    own = owner[...]
    square = (128, 128)
    row, lane = iota(square, 0), iota(square, 1)
    own_col = jnp.sum(jnp.where(row == lane, own, 0), axis=1, keepdims=True)
    least = jnp.min(jnp.where((own_col >> 5) == (own >> 5), own_col, 1 << 20), axis=0, keepdims=True)
    ids = 2 * (own >> 5) + jnp.where(own > least, 1, 0)
    both = jnp.where(
        iota((16, 128), 0) == 0, ids, jnp.where(iota((16, 128), 0) == 1, used[...], 0)
    ).astype(F32).astype(BF16)
    turn = lax.axis_index("bucket") << 2

    def moved(slot):
        return jnp.where(slot < 96, slot, slot ^ turn)

    one = jnp.where(row == moved(lane), 1.0, 0.0).astype(BF16)
    rowid[...] = dot(both, one)[:1].astype(I32)
    wide = (128, POOL * PAGE)
    onehot = jnp.where(iota(wide, 0) == moved(iota(wide, 1) >> 4), 1.0, 0.0).astype(BF16)
    spread[...] = dot(both, onehot)[:8].astype(I32)
    slot = ((row & 15) << 3) + (row >> 4)
    reqcol[...] = jnp.broadcast_to(
        jnp.sum(jnp.where(lane == moved(slot), ids, 0), axis=1, keepdims=True), square
    )
    for copy in copies[2:]:
        copy.wait()
    for b in range(12):
        rows = slice(b * 128, (b + 1) * 128)
        values[rows, :] = pages[rows, KVH * HD :]
    for k in range(NBUC):
        values[(24 + k) * 64 : (25 + k) * 64, :] = arrived[k][:, KVH * HD :]
    store = begin(values, values_out, sem.at[12])
    for b in range(BLOCKS):
        for g in range(KVH):
            cut = slice(g * HD, (g + 1) * HD)
            if b < 12:
                block = pages[b * 128 : (b + 1) * 128, cut]
            else:
                block = jnp.concatenate([one[:, cut] for one in arrived[2 * b - 24 : 2 * b - 22]], axis=0)
            keys[(b * KVH + g) * HD : (b * KVH + g + 1) * HD, :] = block.T
    store.wait()


def leave_body(mig, pages, after, *rest):
    outs, sem = rest[:MOVED], rest[MOVED]
    me = lax.axis_index("bucket")
    copies = []
    for k in range(1, NBUC):
        for j in range(4):
            page = mig[0, (me ^ k) * 4 + j]
            copies.append(
                begin(
                    pages.at[pl.ds(pl.multiple_of(page * PAGE, PAGE), PAGE)],
                    outs[k - 1].at[pl.ds(j * PAGE, PAGE)],
                    sem.at[k * 4 + j],
                )
            )
    for copy in copies:
        copy.wait()


def ahead_body(down_in, base_in, after, down, based, base, turned, sem):
    load = begin(base_in, base, sem.at[0])
    early = begin(down_in.at[:DHALF], down, sem.at[1])
    load.wait()
    for h in range(QH):
        turned[pl.ds(h, REQ, stride=QH), :] = base[:, h * HD : (h + 1) * HD].astype(F32)
    based[...] = turned[...].astype(BF16)
    early.wait()


def adapter_body(rows, early, down_in, up_in, *rest):
    raised, sel, spare, down, up, apart, sem = rest[SOON:]
    loads = [
        begin(down_in.at[DHALF + n * 1024 : DHALF + (n + 1) * 1024], down.at[n * 1024 : (n + 1) * 1024], sem.at[4 + n])
        for n in range(4)
    ]
    load_up = begin(up_in, up, sem.at[8])
    lowered = jnp.zeros((64, 256), F32)
    for n in range(QUART // 128):
        apart[n * 256 : (n + 1) * 256, :] = rows[:, n * 128 : (n + 1) * 128].astype(F32)
    for q in range(4):
        data = jnp.concatenate(
            [apart[pl.ds(n * 256 + q, 64, stride=4), :] for n in range(QUART // 128)], axis=1
        ).astype(BF16)
        if q < 2:
            weights = early[q * QUART : (q + 1) * QUART, :]
        else:
            loads[2 * q - 4].wait()
            loads[2 * q - 3].wait()
            weights = down[(q - 2) * QUART : (q - 1) * QUART, :]
        lowered = lowered + dot(data, weights)
    first = jnp.where(iota((64, 256), 1) == 4 * iota((64, 256), 0), 1.0, 0.0).astype(BF16)
    meta = dot(first, rows[:, QUART:]).astype(I32)
    sel[...] = jnp.sum(
        jnp.where(iota((64, 128), 0) == iota((64, 128), 1), meta[:, 1:2], 0), axis=0, keepdims=True
    )
    chosen = meta[:, 0:1] == (iota((64, 256), 1) >> 6)
    kept = jnp.where(chosen, lowered, 0.0).astype(BF16)
    load_up.wait()
    for n in range(16):
        piece = dot(kept, up[:, n * 256 : (n + 1) * 256])
        spare[pl.ds(2 * n, 64, stride=32), :] = piece[:, :128]
        spare[pl.ds(2 * n + 1, 64, stride=32), :] = piece[:, 128:]
    raised[...] = spare[...].astype(BF16)


def query_body(pos, sel, delta, based, *rest):
    queries, out, packed, sem = rest[MOVED - SOON :]
    for i in range(REQ):
        from_row = pl.multiple_of(pos[0, i] * QH, QH)
        rows = slice(i * QH, (i + 1) * QH)
        queries[rows, :] = (based[rows, :].astype(F32) + delta[pl.ds(from_row, QH), :].astype(F32)).astype(BF16)
    copies = []
    for c in range(2 * NREP):
        from_row = pl.multiple_of(sel[0, c] * QH, QH)
        packed[c * QH : (c + 1) * QH, :] = queries[pl.ds(from_row, QH), :]
        if c % 16 == 15:
            n = c // 16
            copies.append(
                begin(packed.at[n * 512 : (n + 1) * 512], out.at[n * 512 : (n + 1) * 512], sem.at[n])
            )
    for copy in copies:
        copy.wait()


def own_body(queries, new_in, own, new_kv, sem):
    begin(new_in, new_kv, sem.at[0]).wait()
    lane = iota((QH, 128), 1)
    columns = jnp.zeros((QH, 128), F32)
    for i in range(REQ):
        query = queries[i * QH : (i + 1) * QH, :].astype(F32)
        keys = jnp.concatenate(
            [
                jnp.broadcast_to(new_kv[i : i + 1, g * HD : (g + 1) * HD].astype(F32), (8, HD))
                for g in range(KVH)
            ],
            axis=0,
        )
        columns = jnp.where(lane == i, jnp.sum(query * keys, axis=1, keepdims=True), columns)
    padded = jnp.concatenate([columns, jnp.zeros((96, 128), F32)], axis=0)
    own[...] = padded.T[:REQ, :] * SCALE


def merge_pages(blocks):
    lane = iota((QH, 128), 1)
    for step in (8, 4, 2, 1):
        upper = (lane & step) != 0
        merged = []
        for first, second in zip(blocks[:step], blocks[step:]):
            stay = jnp.where(upper, second, first)
            swap = jnp.where(upper, first, second)
            swap = jnp.where(upper, pltpu.roll(swap, step, 1), pltpu.roll(swap, 128 - step, 1))
            merged.append(jnp.maximum(stay, swap))
        blocks = merged
    return blocks[0]


def split3(values):
    high = values.astype(BF16).astype(F32)
    rest = values - high
    middle = rest.astype(BF16).astype(F32)
    return high, middle, rest - middle


def attend_body(
    rowid, spread, reqcol, recv, keys, values_in, packed,
    qf, cs, spare, stats, values, sem, *accs,
):
    load_values = begin(values_in, values, sem.at[0])
    qf[...] = recv[...].astype(F32)
    for acc in accs:
        acc[...] = jnp.zeros_like(acc)
    page8 = iota((8, 128), 1) >> 4
    ids = [rowid[0, p] * QH for p in range(POOL)]
    for b in range(BLOCKS):
        cut = slice(b * 128, (b + 1) * 128)
        for g in range(KVH):
            query = jnp.concatenate(
                [qf[pl.ds(pl.multiple_of(ids[b * 8 + i] + g * 8, 8), 8), :] for i in range(8)], axis=0
            ).astype(BF16)
            found = dot(query, keys[(b * KVH + g) * HD : (b * KVH + g + 1) * HD, :])
            kept = found[0:8]
            for i in range(1, 8):
                kept = jnp.where(page8 == i, found[i * 8 : (i + 1) * 8], kept)
            cs[g * 8 : (g + 1) * 8, cut] = kept

    spot = iota((QH, 128), 1) & 15
    valid, blocks = [], []
    for b in range(BLOCKS):
        cut = slice(b * 128, (b + 1) * 128)
        valid.append(spot < spread[1:2, cut])
        blocks.append(jnp.where(valid[b], cs[:, cut] * SCALE, NEG))
        cs[:, cut] = blocks[b]
    merged = merge_pages(blocks)
    turned = jnp.concatenate([merged] * 4, axis=0).T
    which = reqcol[...] - (iota((128, 128), 1) >> 5)
    tops = jnp.full((128, 128), LOW, F32)
    lines = []
    for n in range(16):
        mine = which == 4 * n
        top = jnp.max(jnp.where(mine, turned, LOW), axis=0, keepdims=True)
        lines.append(top)
        tops = jnp.where(mine, top, tops)
    tops = jnp.maximum(tops, pltpu.roll(tops, 32, 1))
    tops = jnp.maximum(tops, pltpu.roll(tops, 64, 1)).T[:QH, :]
    pieces = jnp.concatenate(split3(tops), axis=0).astype(BF16)
    place = iota((128, 128), 0) - ((iota((128, 128), 1) >> 4) << 4)
    placed = iota((128, 128), 1) - ((iota((128, 128), 0) >> 4) << 4)
    sums = jnp.zeros((QH, 128), F32)
    for b in range(BLOCKS):
        cut = slice(b * 128, (b + 1) * 128)
        spread_tops = dot(pieces, jnp.where(place == b, 1.0, 0.0).astype(BF16))
        top = spread_tops[0:32] + spread_tops[32:64] + spread_tops[64:96]
        weight = jnp.where(valid[b], jnp.exp(cs[:, cut] - top), 0.0).astype(BF16)
        cs[:, cut] = weight.astype(F32)
        sums = sums + dot(weight, jnp.where(placed == b, 1.0, 0.0).astype(BF16))

    load_values.wait()
    for b in range(BLOCKS):
        cut = slice(b * 128, (b + 1) * 128)
        for g in range(KVH):
            weight = cs[g * 8 : (g + 1) * 8, cut]
            spread_weight = jnp.concatenate(
                [jnp.where(page8 == i, weight, 0.0) for i in range(8)], axis=0
            ).astype(BF16)
            found = dot(spread_weight, values[cut, g * HD : (g + 1) * HD])
            for i in range(8):
                at = pl.ds(pl.multiple_of(ids[b * 8 + i] // 4, 8), 8)
                acc = accs[(i % SPLIT) * KVH + g]
                acc[at, :] = acc[at, :] + found[i * 8 : (i + 1) * 8]

    stats[...] = jnp.zeros_like(stats)
    for n, piece in enumerate(split3(jnp.concatenate(lines, axis=0))):
        stats[pl.ds(n, 16, stride=16), :] = piece
        stats[pl.ds(8 + n, 16, stride=16), :] = pltpu.roll(piece, 64, 1)
    member = jnp.where(reqcol[...] == iota((128, 128), 1), 1.0, 0.0)
    sums = dot(sums, member, HIGH)
    spare[...] = jnp.concatenate([sums, jnp.zeros((96, 128), F32)], axis=0).T
    line = spare[pl.ds(0, 32, stride=2), :] + pltpu.roll(spare[pl.ds(1, 32, stride=2), :], 32, 1)
    for n, piece in enumerate(split3(line)):
        stats[pl.ds(3 + n, 32, stride=8), :] = piece
    packed[:, 64:72, :] = stats[...].astype(BF16).reshape(NREP, 8, 128)
    for n in range(4):
        rows = slice(n * 128, (n + 1) * 128)
        groups = [
            sum(accs[k * KVH + g][rows, :] for k in range(SPLIT)).reshape(16, 8, HD)
            for g in range(KVH)
        ]
        part = jnp.concatenate(groups, axis=1).reshape(8, 64, HD)
        packed[n * 8 : (n + 1) * 8, 0:64, :] = part.astype(BF16)


def combine_body(sel, recv, own, new_kv, out, acc, stats, factors):
    stats[...] = recv[:, 64:72, :].astype(F32).reshape(NREP * 8, 128)

    def stat(k):
        read = [stats[pl.ds(3 * k + n, 32, stride=8), :] for n in range(3)]
        return read[0] + read[1] + read[2]

    tops, sums = stat(0), stat(1)
    tops = jnp.concatenate([tops, pltpu.roll(tops, 96, 1)], axis=0)
    sums = jnp.concatenate([sums, pltpu.roll(sums, 96, 1)], axis=0)
    lane = iota((REQ, 128), 1)
    row = iota((REQ, 128), 0)
    head = lane < QH
    own_score = jnp.where(head, own[...], 0.0)
    best = own_score
    picks = [sel[0, 2 * p + s] for s in range(2) for p in range(NREP)]
    for c in range(64):
        best = jnp.where(row == picks[c], jnp.maximum(best, tops[c : c + 1]), best)
    factors[0:32, :] = best
    high = jnp.concatenate([factors[pl.ds(picks[c], 1), :] for c in range(64)], axis=0)
    scaled = jnp.where(iota((64, 128), 1) < QH, jnp.exp(tops - high), 0.0)
    sums = jnp.where(iota((64, 128), 1) < QH, sums, 0.0)
    added = scaled * sums
    total = jnp.exp(own_score - best)
    for c in range(64):
        total = total + jnp.where(row == picks[c], added[c : c + 1], 0.0)
    inverse = 1.0 / total
    own_factor = jnp.where(head, jnp.exp(own_score - best) * inverse, 0.0)
    factors[32:64, :] = inverse
    lines = [
        scaled
        * jnp.concatenate([factors[pl.ds(picks[c] + 32, 1), :] for c in range(64)], axis=0)
    ]
    turned = jnp.concatenate(lines + [own_factor, jnp.zeros((32, 128), F32)], axis=0).T
    turned = turned[:QH, :]
    for i in range(REQ):
        values = jnp.concatenate(
            [
                jnp.broadcast_to(
                    new_kv[i : i + 1, (KVH + g) * HD : (KVH + g + 1) * HD].astype(F32), (8, HD)
                )
                for g in range(KVH)
            ],
            axis=0,
        )
        acc[i * QH : (i + 1) * QH, :] = turned[:, 64 + i : 65 + i] * values
    for c in range(64):
        s, p = c // 32, c % 32
        at = pl.ds(pl.multiple_of(picks[c] * QH, QH), QH)
        given = recv[p, s * QH : (s + 1) * QH, :].astype(F32)
        acc[at, :] = acc[at, :] + turned[:, c : c + 1] * given
    for h in range(QH):
        out[:, h * HD : (h + 1) * HD] = acc[pl.ds(h, REQ, stride=QH), :].astype(BF16)


def exchange(values, axis):
    return lax.all_to_all(values, axis, split_axis=0, concat_axis=0, tiled=True)


def shards(
    hidden,
    base_query_rows,
    new_kv,
    adapter_down_matrix,
    adapter_up_matrix,
    holder,
    adapter_slot,
    kv_pages,
    mig_pages,
    page_owner,
    page_used,
):
    owner = in_hbm(page_owner.reshape(1, POOL))
    outgoing, pos = call(
        dispatch_body,
        [pltpu.HBM((256, WIDE), BF16), shape((1, 128), I32)],
        scratch=[
            pltpu.VMEM((REQ, 4 * QUART), BF16),
            pltpu.VMEM((1, REQ), I32),
            pltpu.VMEM((1, REQ), I32),
            pltpu.VMEM((1, POOL), I32),
            pltpu.VMEM((256, WIDE), BF16),
            sems(8),
        ],
        ins=[ANY] * 4,
        out_specs=[ANY, VM],
        moved=2 << 20,
    )(in_hbm(hidden), in_hbm(holder.reshape(1, REQ)), in_hbm(adapter_slot.reshape(1, REQ)), owner)
    rows_in = exchange(outgoing.reshape(NREP, 8, WIDE), "replica")

    down = in_hbm(adapter_down_matrix)
    flat_pages = in_hbm(kv_pages.reshape(96 * PAGE, 1024))
    mig = mig_pages.reshape(1, 32)
    leaving = call(
        leave_body,
        [pltpu.VMEM((64, 1024), BF16)] * MOVED,
        scratch=[sems(32)],
        ins=[SM] + [ANY] * 2,
        moved=2 << 20,
    )(mig, flat_pages, pos)
    arrived = [
        in_hbm(lax.ppermute(one, "bucket", [(s, s ^ (k + 1)) for s in range(NBUC)]))
        for k, one in enumerate(leaving)
    ]
    early, based = call(
        ahead_body,
        [pltpu.VMEM((DHALF, 256), BF16), pltpu.VMEM((REQ * QH, HD), BF16)],
        scratch=[pltpu.VMEM((REQ, QH * HD), BF16), pltpu.VMEM((REQ * QH, HD), F32), sems(2)],
        ins=[ANY] * 3,
        moved=5 << 20,
    )(down, in_hbm(base_query_rows), arrived[0])

    raised, sel = call(
        adapter_body,
        [pltpu.VMEM((2048, 128), BF16), shape((1, 128), I32)],
        scratch=[
            pltpu.VMEM((2048, 128), F32),
            pltpu.VMEM((DHALF, 256), BF16),
            pltpu.VMEM(adapter_up_matrix.shape, BF16),
            pltpu.VMEM((2 * QUART, 128), F32),
            sems(9),
        ],
        ins=[VM, VM] + [ANY] * (2 + SOON),
        flops=1 << 30,
        moved=8 << 20,
    )(
        in_vmem(rows_in.reshape(256, WIDE)),
        in_vmem(early),
        down,
        in_hbm(adapter_up_matrix),
        *arrived[:SOON],
    )
    returned = exchange(raised.reshape(NREP, 64, 128), "replica")
    queries, asked = call(
        query_body,
        [pltpu.VMEM((REQ * QH, HD), BF16), pltpu.HBM((2048, 128), BF16)],
        scratch=[pltpu.VMEM((2048, 128), BF16), sems(4)],
        ins=[SM, SM, VM, VM] + [ANY] * (MOVED - SOON),
        out_specs=[VM, ANY],
    )(pos, sel, in_vmem(returned.reshape(2048, 128)), in_vmem(based), *arrived[SOON:])
    recv = exchange(asked.reshape(NREP, 64, 128), "replica")
    own, fresh = call(
        own_body,
        [pltpu.VMEM((REQ, 128), F32), pltpu.VMEM(new_kv.shape, BF16)],
        scratch=[sems(1)],
        ins=[VM, ANY],
    )(in_vmem(queries), in_hbm(new_kv))
    rowid, spread, reqcol, keys, values = call(
        prepare_body,
        [
            shape((1, 128), I32),
            pltpu.VMEM((8, POOL * PAGE), I32),
            pltpu.VMEM((128, 128), I32),
            pltpu.VMEM((BLOCKS * KVH * HD, 128), BF16),
            pltpu.HBM((POOL * PAGE, KVH * HD), BF16),
        ],
        scratch=[
            pltpu.VMEM((1, POOL), I32),
            pltpu.VMEM((1, POOL), I32),
            pltpu.VMEM((96 * PAGE, 1024), BF16),
            pltpu.VMEM((32 * PAGE, 1024), BF16),
            pltpu.VMEM((POOL * PAGE, KVH * HD), BF16),
            sems(17),
        ],
        ins=[SM] + [ANY] * (4 + MOVED),
        out_specs=[VM] * 4 + [ANY],
        moved=8 << 20,
    )(
        mig,
        owner,
        in_hbm(page_used.reshape(1, POOL)),
        flat_pages,
        own,
        *arrived,
    )

    (partial,) = call(
        attend_body,
        [pltpu.VMEM((NREP, CROWS, 128), BF16)],
        scratch=[
            pltpu.VMEM((2048, 128), F32),
            pltpu.VMEM((QH, POOL * PAGE), F32),
            pltpu.VMEM((128, 128), F32),
            pltpu.VMEM((256, 128), F32),
            pltpu.VMEM((POOL * PAGE, KVH * HD), BF16),
            sems(1),
        ]
        + [pltpu.VMEM((512, 128), F32)] * (SPLIT * KVH),
        ins=[SM] + [VM] * 4 + [ANY],
        flops=1 << 29,
        moved=6 << 20,
    )(
        rowid,
        in_vmem(spread),
        in_vmem(reqcol),
        in_vmem(recv.reshape(2048, 128)),
        in_vmem(keys),
        in_hbm(values),
    )
    parts = exchange(partial, "replica")

    return call(
        combine_body,
        [shape((REQ, QH * HD), BF16)],
        scratch=[
            pltpu.VMEM((REQ * QH, HD), F32),
            pltpu.VMEM((256, 128), F32),
            pltpu.VMEM((64, 128), F32),
        ],
        ins=[SM, VM, VM, VM],
    )(sel, in_vmem(parts), in_vmem(own), in_vmem(fresh))[0]


def solution(mesh):
    rows = P(("bucket", "replica"), None)
    flat = P(("bucket", "replica"))
    placed = (
        rows,
        rows,
        rows,
        P(None, ("bucket", "replica")),
        rows,
        rows,
        flat,
        P(("bucket", "replica"), None, None),
        flat,
        flat,
        flat,
    )
    return jax.shard_map(
        shards, mesh=mesh, in_specs=placed, out_specs=rows, check_vma=False
    )
```

```python
import jax
import jax.numpy as jnp
from jax import lax
from jax.experimental import pallas as pl
from jax.experimental.pallas import tpu as pltpu
from jax.sharding import PartitionSpec as P

QH = 32
KVH = 4
HD = 128
RANK = 64
PAGE = 16
REQ = 32
NREP = 32
NBUC = 8
POOL = 128
QUART = 2048
WIDE = QUART + 128
BLOCKS = 16
CROWS = 72
DHALF = 4096
MOVED = 7
SOON = 7
SPLIT = 1
SCALE = HD ** -0.5
LOW = -3e38
NEG = -1e30
HIGH = lax.Precision.HIGHEST
F32 = jnp.float32
BF16 = jnp.bfloat16
I32 = jnp.int32
VM = pl.BlockSpec(memory_space=pltpu.VMEM)
ANY = pl.BlockSpec(memory_space=pl.ANY)
SM = pl.BlockSpec(memory_space=pltpu.SMEM)


def iota(shape, axis):
    return lax.broadcasted_iota(I32, shape, axis)


def dot(left, right, precision=None):
    return jnp.dot(left, right, preferred_element_type=F32, precision=precision)


def call(body, outs, scratch=(), ins=None, out_specs=None, mib=24, flops=1 << 20, moved=1 << 20):
    return pl.pallas_call(
        body,
        out_shape=tuple(outs),
        in_specs=ins,
        out_specs=tuple(out_specs or [VM] * len(outs)),
        scratch_shapes=list(scratch),
        compiler_params=pltpu.CompilerParams(vmem_limit_bytes=mib << 20),
        cost_estimate=pl.CostEstimate(flops=flops, bytes_accessed=moved, transcendentals=0),
    )


def in_hbm(values):
    return pltpu.with_memory_space_constraint(values, pltpu.HBM)


def in_vmem(values):
    return pltpu.with_memory_space_constraint(values, pltpu.VMEM)


def begin(source, target, sem):
    copy = pltpu.make_async_copy(source, target, sem)
    copy.start()
    return copy


def sems(count):
    return pltpu.SemaphoreType.DMA((count,))


def shape(dims, kind):
    return jax.ShapeDtypeStruct(dims, kind)


def dispatch_body(hidden_in, holder_in, slot_in, owner_in, out, pos, hidden, holder, slot, owner, made, sem):
    small = [
        begin(source, target, sem.at[n])
        for n, (source, target) in enumerate(
            ((holder_in, holder), (slot_in, slot), (owner_in, owner))
        )
    ]
    large = begin(hidden_in, hidden, sem.at[3])
    for copy in small:
        copy.wait()
    square = (REQ, REQ)
    col = jnp.sum(
        jnp.where(iota(square, 0) == iota(square, 1), holder[...], 0), axis=1, keepdims=True
    )
    col4 = jnp.concatenate([col] * 4, axis=0)
    square = (128, 128)
    target = jnp.sum(jnp.where(iota(square, 0) == iota(square, 1), col4, 0), axis=0, keepdims=True)
    earlier = (col == target) & (iota((REQ, 128), 0) < (iota((REQ, 128), 1) & 31))
    rank = jnp.sum(jnp.where(earlier, 1, 0), axis=0, keepdims=True)
    place = 2 * target + rank
    pos[...] = place
    full = (256, 128)
    row, lane = iota(full, 0), iota(full, 1)
    at_place = (row >> 2) == place
    onehot = jnp.where(at_place & ((row & 3) == (lane >> 5)), 1.0, 0.0).astype(BF16)
    large.wait()
    stacked = jnp.concatenate([hidden[:, q * QUART : (q + 1) * QUART] for q in range(4)], axis=0)
    copies = []
    for n in range(4):
        rows = slice(n * 64, (n + 1) * 64)
        made[rows, :QUART] = dot(onehot[rows], stacked).astype(BF16)
        copies.append(begin(made.at[rows, :QUART], out.at[rows, :QUART], sem.at[4 + n]))
    slot_col = jnp.sum(jnp.where(at_place[:, :REQ], slot[...], 0), axis=1, keepdims=True)
    own = owner[...]
    here = (own >> 5) == (row >> 3)
    local = own & 31
    least = jnp.min(jnp.where(here, local, 99), axis=1, keepdims=True)
    most = jnp.max(jnp.where(here, local, -1), axis=1, keepdims=True)
    second = ((row >> 2) & 1) == 1
    chosen = jnp.where(second, most, least)
    meta = jnp.where(lane == 0, slot_col, jnp.where(lane == 1, chosen, 0))
    made[:, QUART:] = meta.astype(F32).astype(BF16)
    copies.append(begin(made.at[:, QUART:], out.at[:, QUART:], sem.at[8]))
    for copy in copies:
        copy.wait()


def prepare_body(mig, owner_in, used_in, pages_in, after, *rest):
    given, outs, scratch = rest[:MOVED], rest[MOVED : MOVED + 5], rest[MOVED + 5 :]
    rowid, spread, reqcol, keys, values_out = outs
    owner, used, pages, pieces, values, sem = scratch
    copies = [
        begin(source, target, sem.at[n])
        for n, (source, target) in enumerate(
            ((owner_in, owner), (used_in, used), (pages_in, pages))
        )
    ]
    arrived = [pieces.at[k * 64 : (k + 1) * 64] for k in range(NBUC)]
    copies += [begin(given[k - 1], arrived[k], sem.at[4 + k]) for k in range(1, NBUC)]
    for j in range(4):
        page = mig[0, lax.axis_index("bucket") * 4 + j]
        rows = pl.ds(pl.multiple_of(page * PAGE, PAGE), PAGE)
        copies.append(begin(pages_in.at[rows], pieces.at[pl.ds(j * PAGE, PAGE)], sem.at[13 + j]))
    copies[0].wait()
    copies[1].wait()
    own = owner[...]
    square = (128, 128)
    row, lane = iota(square, 0), iota(square, 1)
    own_col = jnp.sum(jnp.where(row == lane, own, 0), axis=1, keepdims=True)
    least = jnp.min(jnp.where((own_col >> 5) == (own >> 5), own_col, 1 << 20), axis=0, keepdims=True)
    ids = 2 * (own >> 5) + jnp.where(own > least, 1, 0)
    both = jnp.where(
        iota((16, 128), 0) == 0, ids, jnp.where(iota((16, 128), 0) == 1, used[...], 0)
    ).astype(F32).astype(BF16)
    turn = lax.axis_index("bucket") << 2

    def moved(slot):
        return jnp.where(slot < 96, slot, slot ^ turn)

    one = jnp.where(row == moved(lane), 1.0, 0.0).astype(BF16)
    rowid[...] = dot(both, one)[:1].astype(I32)
    wide = (128, POOL * PAGE)
    onehot = jnp.where(iota(wide, 0) == moved(iota(wide, 1) >> 4), 1.0, 0.0).astype(BF16)
    spread[...] = dot(both, onehot)[:8].astype(I32)
    slot = ((row & 15) << 3) + (row >> 4)
    reqcol[...] = jnp.broadcast_to(
        jnp.sum(jnp.where(lane == moved(slot), ids, 0), axis=1, keepdims=True), square
    )
    for copy in copies[2:]:
        copy.wait()
    for b in range(12):
        rows = slice(b * 128, (b + 1) * 128)
        values[rows, :] = pages[rows, KVH * HD :]
    for k in range(NBUC):
        values[(24 + k) * 64 : (25 + k) * 64, :] = arrived[k][:, KVH * HD :]
    store = begin(values, values_out, sem.at[12])
    for b in range(BLOCKS):
        for g in range(KVH):
            cut = slice(g * HD, (g + 1) * HD)
            if b < 12:
                block = pages[b * 128 : (b + 1) * 128, cut]
            else:
                block = jnp.concatenate([one[:, cut] for one in arrived[2 * b - 24 : 2 * b - 22]], axis=0)
            keys[(b * KVH + g) * HD : (b * KVH + g + 1) * HD, :] = block.T
    store.wait()


def leave_body(mig, pages, after, *rest):
    outs, sem = rest[:MOVED], rest[MOVED]
    me = lax.axis_index("bucket")
    copies = []
    for k in range(1, NBUC):
        for j in range(4):
            page = mig[0, (me ^ k) * 4 + j]
            copies.append(
                begin(
                    pages.at[pl.ds(pl.multiple_of(page * PAGE, PAGE), PAGE)],
                    outs[k - 1].at[pl.ds(j * PAGE, PAGE)],
                    sem.at[k * 4 + j],
                )
            )
    for copy in copies:
        copy.wait()


def ahead_body(down_in, base_in, after, down, based, base, turned, sem):
    load = begin(base_in, base, sem.at[0])
    early = begin(down_in.at[:DHALF], down, sem.at[1])
    load.wait()
    for h in range(QH):
        turned[pl.ds(h, REQ, stride=QH), :] = base[:, h * HD : (h + 1) * HD].astype(F32)
    based[...] = turned[...].astype(BF16)
    early.wait()


def adapter_body(rows, early, down_in, up_in, *rest):
    raised, sel, spare, down, up, apart, sem = rest[SOON:]
    loads = [
        begin(down_in.at[DHALF + n * 1024 : DHALF + (n + 1) * 1024], down.at[n * 1024 : (n + 1) * 1024], sem.at[4 + n])
        for n in range(4)
    ]
    load_up = begin(up_in, up, sem.at[8])
    lowered = jnp.zeros((64, 256), F32)
    for n in range(QUART // 128):
        apart[n * 256 : (n + 1) * 256, :] = rows[:, n * 128 : (n + 1) * 128].astype(F32)
    for q in range(4):
        data = jnp.concatenate(
            [apart[pl.ds(n * 256 + q, 64, stride=4), :] for n in range(QUART // 128)], axis=1
        ).astype(BF16)
        if q < 2:
            weights = early[q * QUART : (q + 1) * QUART, :]
        else:
            loads[2 * q - 4].wait()
            loads[2 * q - 3].wait()
            weights = down[(q - 2) * QUART : (q - 1) * QUART, :]
        lowered = lowered + dot(data, weights)
    first = jnp.where(iota((64, 256), 1) == 4 * iota((64, 256), 0), 1.0, 0.0).astype(BF16)
    meta = dot(first, rows[:, QUART:]).astype(I32)
    sel[...] = jnp.sum(
        jnp.where(iota((64, 128), 0) == iota((64, 128), 1), meta[:, 1:2], 0), axis=0, keepdims=True
    )
    chosen = meta[:, 0:1] == (iota((64, 256), 1) >> 6)
    kept = jnp.where(chosen, lowered, 0.0).astype(BF16)
    load_up.wait()
    for n in range(16):
        piece = dot(kept, up[:, n * 256 : (n + 1) * 256])
        spare[pl.ds(2 * n, 64, stride=32), :] = piece[:, :128]
        spare[pl.ds(2 * n + 1, 64, stride=32), :] = piece[:, 128:]
    raised[...] = spare[...].astype(BF16)


def query_body(pos, sel, delta, based, *rest):
    queries, out, packed, sem = rest[MOVED - SOON :]
    for i in range(REQ):
        from_row = pl.multiple_of(pos[0, i] * QH, QH)
        rows = slice(i * QH, (i + 1) * QH)
        queries[rows, :] = (based[rows, :].astype(F32) + delta[pl.ds(from_row, QH), :].astype(F32)).astype(BF16)
    copies = []
    for c in range(2 * NREP):
        from_row = pl.multiple_of(sel[0, c] * QH, QH)
        packed[c * QH : (c + 1) * QH, :] = queries[pl.ds(from_row, QH), :]
        if c % 16 == 15:
            n = c // 16
            copies.append(
                begin(packed.at[n * 512 : (n + 1) * 512], out.at[n * 512 : (n + 1) * 512], sem.at[n])
            )
    for copy in copies:
        copy.wait()


def own_body(queries, new_in, own, new_kv, sem):
    begin(new_in, new_kv, sem.at[0]).wait()
    lane = iota((QH, 128), 1)
    columns = jnp.zeros((QH, 128), F32)
    for i in range(REQ):
        query = queries[i * QH : (i + 1) * QH, :].astype(F32)
        keys = jnp.concatenate(
            [
                jnp.broadcast_to(new_kv[i : i + 1, g * HD : (g + 1) * HD].astype(F32), (8, HD))
                for g in range(KVH)
            ],
            axis=0,
        )
        columns = jnp.where(lane == i, jnp.sum(query * keys, axis=1, keepdims=True), columns)
    padded = jnp.concatenate([columns, jnp.zeros((96, 128), F32)], axis=0)
    own[...] = padded.T[:REQ, :] * SCALE


def merge_pages(blocks):
    lane = iota((QH, 128), 1)
    for step in (8, 4, 2, 1):
        upper = (lane & step) != 0
        merged = []
        for first, second in zip(blocks[:step], blocks[step:]):
            stay = jnp.where(upper, second, first)
            swap = jnp.where(upper, first, second)
            swap = jnp.where(upper, pltpu.roll(swap, step, 1), pltpu.roll(swap, 128 - step, 1))
            merged.append(jnp.maximum(stay, swap))
        blocks = merged
    return blocks[0]


def split3(values):
    high = values.astype(BF16).astype(F32)
    rest = values - high
    middle = rest.astype(BF16).astype(F32)
    return high, middle, rest - middle


def attend_body(
    rowid, spread, reqcol, recv, keys, values_in, packed,
    qf, cs, spare, stats, values, sem, *accs,
):
    load_values = begin(values_in, values, sem.at[0])
    qf[...] = recv[...].astype(F32)
    for acc in accs:
        acc[...] = jnp.zeros_like(acc)
    page8 = iota((8, 128), 1) >> 4
    ids = [rowid[0, p] * QH for p in range(POOL)]
    for b in range(BLOCKS):
        cut = slice(b * 128, (b + 1) * 128)
        for g in range(KVH):
            query = jnp.concatenate(
                [qf[pl.ds(pl.multiple_of(ids[b * 8 + i] + g * 8, 8), 8), :] for i in range(8)], axis=0
            ).astype(BF16)
            found = dot(query, keys[(b * KVH + g) * HD : (b * KVH + g + 1) * HD, :])
            kept = found[0:8]
            for i in range(1, 8):
                kept = jnp.where(page8 == i, found[i * 8 : (i + 1) * 8], kept)
            cs[g * 8 : (g + 1) * 8, cut] = kept

    spot = iota((QH, 128), 1) & 15
    valid, blocks = [], []
    for b in range(BLOCKS):
        cut = slice(b * 128, (b + 1) * 128)
        valid.append(spot < spread[1:2, cut])
        blocks.append(jnp.where(valid[b], cs[:, cut] * SCALE, NEG))
        cs[:, cut] = blocks[b]
    merged = merge_pages(blocks)
    turned = jnp.concatenate([merged] * 4, axis=0).T
    which = reqcol[...] - (iota((128, 128), 1) >> 5)
    tops = jnp.full((128, 128), LOW, F32)
    lines = []
    for n in range(16):
        mine = which == 4 * n
        top = jnp.max(jnp.where(mine, turned, LOW), axis=0, keepdims=True)
        lines.append(top)
        tops = jnp.where(mine, top, tops)
    tops = jnp.maximum(tops, pltpu.roll(tops, 32, 1))
    tops = jnp.maximum(tops, pltpu.roll(tops, 64, 1)).T[:QH, :]
    pieces = jnp.concatenate(split3(tops), axis=0).astype(BF16)
    place = iota((128, 128), 0) - ((iota((128, 128), 1) >> 4) << 4)
    placed = iota((128, 128), 1) - ((iota((128, 128), 0) >> 4) << 4)
    sums = jnp.zeros((QH, 128), F32)
    for b in range(BLOCKS):
        cut = slice(b * 128, (b + 1) * 128)
        spread_tops = dot(pieces, jnp.where(place == b, 1.0, 0.0).astype(BF16))
        top = spread_tops[0:32] + spread_tops[32:64] + spread_tops[64:96]
        weight = jnp.where(valid[b], jnp.exp(cs[:, cut] - top), 0.0).astype(BF16)
        cs[:, cut] = weight.astype(F32)
        sums = sums + dot(weight, jnp.where(placed == b, 1.0, 0.0).astype(BF16))

    load_values.wait()
    for b in range(BLOCKS):
        cut = slice(b * 128, (b + 1) * 128)
        for g in range(KVH):
            weight = cs[g * 8 : (g + 1) * 8, cut]
            spread_weight = jnp.concatenate(
                [jnp.where(page8 == i, weight, 0.0) for i in range(8)], axis=0
            ).astype(BF16)
            found = dot(spread_weight, values[cut, g * HD : (g + 1) * HD])
            for i in range(8):
                at = pl.ds(pl.multiple_of(ids[b * 8 + i] // 4, 8), 8)
                acc = accs[(i % SPLIT) * KVH + g]
                acc[at, :] = acc[at, :] + found[i * 8 : (i + 1) * 8]

    stats[...] = jnp.zeros_like(stats)
    for n, piece in enumerate(split3(jnp.concatenate(lines, axis=0))):
        stats[pl.ds(n, 16, stride=16), :] = piece
        stats[pl.ds(8 + n, 16, stride=16), :] = pltpu.roll(piece, 64, 1)
    member = jnp.where(reqcol[...] == iota((128, 128), 1), 1.0, 0.0)
    sums = dot(sums, member, HIGH)
    spare[...] = jnp.concatenate([sums, jnp.zeros((96, 128), F32)], axis=0).T
    line = spare[pl.ds(0, 32, stride=2), :] + pltpu.roll(spare[pl.ds(1, 32, stride=2), :], 32, 1)
    for n, piece in enumerate(split3(line)):
        stats[pl.ds(3 + n, 32, stride=8), :] = piece
    packed[:, 64:72, :] = stats[...].astype(BF16).reshape(NREP, 8, 128)
    for n in range(4):
        rows = slice(n * 128, (n + 1) * 128)
        groups = [
            sum(accs[k * KVH + g][rows, :] for k in range(SPLIT)).reshape(16, 8, HD)
            for g in range(KVH)
        ]
        part = jnp.concatenate(groups, axis=1).reshape(8, 64, HD)
        packed[n * 8 : (n + 1) * 8, 0:64, :] = part.astype(BF16)


def combine_body(sel, recv, own, new_kv, out, acc, stats, factors):
    stats[...] = recv[:, 64:72, :].astype(F32).reshape(NREP * 8, 128)

    def stat(k):
        read = [stats[pl.ds(3 * k + n, 32, stride=8), :] for n in range(3)]
        return read[0] + read[1] + read[2]

    tops, sums = stat(0), stat(1)
    tops = jnp.concatenate([tops, pltpu.roll(tops, 96, 1)], axis=0)
    sums = jnp.concatenate([sums, pltpu.roll(sums, 96, 1)], axis=0)
    lane = iota((REQ, 128), 1)
    row = iota((REQ, 128), 0)
    head = lane < QH
    own_score = jnp.where(head, own[...], 0.0)
    best = own_score
    picks = [sel[0, 2 * p + s] for s in range(2) for p in range(NREP)]
    for c in range(64):
        best = jnp.where(row == picks[c], jnp.maximum(best, tops[c : c + 1]), best)
    factors[0:32, :] = best
    high = jnp.concatenate([factors[pl.ds(picks[c], 1), :] for c in range(64)], axis=0)
    scaled = jnp.where(iota((64, 128), 1) < QH, jnp.exp(tops - high), 0.0)
    sums = jnp.where(iota((64, 128), 1) < QH, sums, 0.0)
    added = scaled * sums
    total = jnp.exp(own_score - best)
    for c in range(64):
        total = total + jnp.where(row == picks[c], added[c : c + 1], 0.0)
    inverse = 1.0 / total
    own_factor = jnp.where(head, jnp.exp(own_score - best) * inverse, 0.0)
    factors[32:64, :] = inverse
    lines = [
        scaled
        * jnp.concatenate([factors[pl.ds(picks[c] + 32, 1), :] for c in range(64)], axis=0)
    ]
    turned = jnp.concatenate(lines + [own_factor, jnp.zeros((32, 128), F32)], axis=0).T
    turned = turned[:QH, :]
    for i in range(REQ):
        values = jnp.concatenate(
            [
                jnp.broadcast_to(
                    new_kv[i : i + 1, (KVH + g) * HD : (KVH + g + 1) * HD].astype(F32), (8, HD)
                )
                for g in range(KVH)
            ],
            axis=0,
        )
        acc[i * QH : (i + 1) * QH, :] = turned[:, 64 + i : 65 + i] * values
    for c in range(64):
        s, p = c // 32, c % 32
        at = pl.ds(pl.multiple_of(picks[c] * QH, QH), QH)
        given = recv[p, s * QH : (s + 1) * QH, :].astype(F32)
        acc[at, :] = acc[at, :] + turned[:, c : c + 1] * given
    for h in range(QH):
        out[:, h * HD : (h + 1) * HD] = acc[pl.ds(h, REQ, stride=QH), :].astype(BF16)


def exchange(values, axis):
    return lax.all_to_all(values, axis, split_axis=0, concat_axis=0, tiled=True)


def shards(
    hidden,
    base_query_rows,
    new_kv,
    adapter_down_matrix,
    adapter_up_matrix,
    holder,
    adapter_slot,
    kv_pages,
    mig_pages,
    page_owner,
    page_used,
):
    owner = in_hbm(page_owner.reshape(1, POOL))
    outgoing, pos = call(
        dispatch_body,
        [pltpu.HBM((256, WIDE), BF16), shape((1, 128), I32)],
        scratch=[
            pltpu.VMEM((REQ, 4 * QUART), BF16),
            pltpu.VMEM((1, REQ), I32),
            pltpu.VMEM((1, REQ), I32),
            pltpu.VMEM((1, POOL), I32),
            pltpu.VMEM((256, WIDE), BF16),
            sems(9),
        ],
        ins=[ANY] * 4,
        out_specs=[ANY, VM],
        moved=2 << 20,
    )(in_hbm(hidden), in_hbm(holder.reshape(1, REQ)), in_hbm(adapter_slot.reshape(1, REQ)), owner)
    rows_in = exchange(outgoing.reshape(NREP, 8, WIDE), "replica")

    down = in_hbm(adapter_down_matrix)
    flat_pages = in_hbm(kv_pages.reshape(96 * PAGE, 1024))
    mig = mig_pages.reshape(1, 32)
    leaving = call(
        leave_body,
        [pltpu.VMEM((64, 1024), BF16)] * MOVED,
        scratch=[sems(32)],
        ins=[SM] + [ANY] * 2,
        moved=2 << 20,
    )(mig, flat_pages, pos)
    arrived = [
        in_hbm(lax.ppermute(one, "bucket", [(s, s ^ (k + 1)) for s in range(NBUC)]))
        for k, one in enumerate(leaving)
    ]
    early, based = call(
        ahead_body,
        [pltpu.VMEM((DHALF, 256), BF16), pltpu.VMEM((REQ * QH, HD), BF16)],
        scratch=[pltpu.VMEM((REQ, QH * HD), BF16), pltpu.VMEM((REQ * QH, HD), F32), sems(2)],
        ins=[ANY] * 3,
        moved=5 << 20,
    )(down, in_hbm(base_query_rows), arrived[0])

    raised, sel = call(
        adapter_body,
        [pltpu.VMEM((2048, 128), BF16), shape((1, 128), I32)],
        scratch=[
            pltpu.VMEM((2048, 128), F32),
            pltpu.VMEM((DHALF, 256), BF16),
            pltpu.VMEM(adapter_up_matrix.shape, BF16),
            pltpu.VMEM((2 * QUART, 128), F32),
            sems(9),
        ],
        ins=[VM, VM] + [ANY] * (2 + SOON),
        flops=1 << 30,
        moved=8 << 20,
    )(
        in_vmem(rows_in.reshape(256, WIDE)),
        in_vmem(early),
        down,
        in_hbm(adapter_up_matrix),
        *arrived[:SOON],
    )
    returned = exchange(raised.reshape(NREP, 64, 128), "replica")
    queries, asked = call(
        query_body,
        [pltpu.VMEM((REQ * QH, HD), BF16), pltpu.HBM((2048, 128), BF16)],
        scratch=[pltpu.VMEM((2048, 128), BF16), sems(4)],
        ins=[SM, SM, VM, VM] + [ANY] * (MOVED - SOON),
        out_specs=[VM, ANY],
    )(pos, sel, in_vmem(returned.reshape(2048, 128)), in_vmem(based), *arrived[SOON:])
    recv = exchange(asked.reshape(NREP, 64, 128), "replica")
    own, fresh = call(
        own_body,
        [pltpu.VMEM((REQ, 128), F32), pltpu.VMEM(new_kv.shape, BF16)],
        scratch=[sems(1)],
        ins=[VM, ANY],
    )(in_vmem(queries), in_hbm(new_kv))
    rowid, spread, reqcol, keys, values = call(
        prepare_body,
        [
            shape((1, 128), I32),
            pltpu.VMEM((8, POOL * PAGE), I32),
            pltpu.VMEM((128, 128), I32),
            pltpu.VMEM((BLOCKS * KVH * HD, 128), BF16),
            pltpu.HBM((POOL * PAGE, KVH * HD), BF16),
        ],
        scratch=[
            pltpu.VMEM((1, POOL), I32),
            pltpu.VMEM((1, POOL), I32),
            pltpu.VMEM((96 * PAGE, 1024), BF16),
            pltpu.VMEM((32 * PAGE, 1024), BF16),
            pltpu.VMEM((POOL * PAGE, KVH * HD), BF16),
            sems(17),
        ],
        ins=[SM] + [ANY] * (4 + MOVED),
        out_specs=[VM] * 4 + [ANY],
        moved=8 << 20,
    )(
        mig,
        owner,
        in_hbm(page_used.reshape(1, POOL)),
        flat_pages,
        own,
        *arrived,
    )

    (partial,) = call(
        attend_body,
        [pltpu.VMEM((NREP, CROWS, 128), BF16)],
        scratch=[
            pltpu.VMEM((2048, 128), F32),
            pltpu.VMEM((QH, POOL * PAGE), F32),
            pltpu.VMEM((128, 128), F32),
            pltpu.VMEM((256, 128), F32),
            pltpu.VMEM((POOL * PAGE, KVH * HD), BF16),
            sems(1),
        ]
        + [pltpu.VMEM((512, 128), F32)] * (SPLIT * KVH),
        ins=[SM] + [VM] * 4 + [ANY],
        flops=1 << 29,
        moved=6 << 20,
    )(
        rowid,
        in_vmem(spread),
        in_vmem(reqcol),
        in_vmem(recv.reshape(2048, 128)),
        in_vmem(keys),
        in_hbm(values),
    )
    parts = exchange(partial, "replica")

    return call(
        combine_body,
        [shape((REQ, QH * HD), BF16)],
        scratch=[
            pltpu.VMEM((REQ * QH, HD), F32),
            pltpu.VMEM((256, 128), F32),
            pltpu.VMEM((64, 128), F32),
        ],
        ins=[SM, VM, VM, VM],
    )(sel, in_vmem(parts), in_vmem(own), in_vmem(fresh))[0]


def solution(mesh):
    rows = P(("bucket", "replica"), None)
    flat = P(("bucket", "replica"))
    placed = (
        rows,
        rows,
        rows,
        P(None, ("bucket", "replica")),
        rows,
        rows,
        flat,
        P(("bucket", "replica"), None, None),
        flat,
        flat,
        flat,
    )
    return jax.shard_map(
        shards, mesh=mesh, in_specs=placed, out_specs=rows, check_vma=False
    )
```
